32 devices in a mesh: row: 4 (over z), col: 8 (over y, x, core).
Axes of the slice: x: 2, y: 2, z: 4, core: 2. Of those that a mesh axis runs over, the one named last changes fastest.
Arguments:
- recorded: bfloat16 [512, 64, 3072], P(('row', 'col')), may hold values from -6 to 6
- seg_count: int32 [32], P(('row', 'col')), may hold values from 0 to 16, as said below
- slot_station: int32 [512], P(('row', 'col')), may hold values from 0 to 255, as said below
- window_mask: int32 [256, 64], P(('row', 'col')), may hold values from 0 to 1, as said below
Outputs:
- cross_real: bfloat16 [256, 256, 384], P('row', 'col')
- cross_imag: bfloat16 [256, 256, 384], P('row', 'col')
The draws below stay inside these ranges and needn't reach their ends.
Inputs may be any that keep to these rules, and one draw needn't show every extreme that they name: `seg_count`: recorder d = r * 8 + c serves row r of the grid; in every row exactly half of the 8 recorders have 16 live slots and the others none. `slot_station`: the live slots of the recorders of row r name each station of r * 64 to (r + 1) * 64 - 1 exactly once; a recorder's live slots name 2 or no stations of each owner (stations with equal s // 8); dead slots name arbitrary stations. `window_mask`: A station's invalid windows form one cyclic run of 0 to 64 windows.
All inputs are finite; a program needn't handle non-finite values.
Results may differ from the reference program's by a relative error of at most 0.0066.
Values may be sent and summed in bfloat16 or wider, within the bound.
A program may use at most 128 MiB of HBM per device.

```python
import math
import jax
import jax.numpy as jnp
from jax import lax

F = 384
L = 3072
F0 = 13
BAND = 64
S_DEV = 8
W = 64
RECS = 8
GRID_ROWS = 4
R_ST = 16
S_ROW = 64
NCB = 32
S = 256
SLOTS = 512


def recorder_layout(key):
    half = RECS // 2
    pairs = S_DEV // 2

    def one_row(row):
        row_key = jax.random.fold_in(jax.random.fold_in(key, 7001), row)
        busy = jax.random.permutation(jax.random.fold_in(row_key, 1), RECS).astype(jnp.int32)
        owner_keys = jax.random.split(jax.random.fold_in(row_key, 2), RECS)
        orders = jax.vmap(lambda k: jax.random.permutation(k, S_DEV))(owner_keys).astype(jnp.int32)
        owners = jnp.arange(RECS, dtype=jnp.int32)
        which = jnp.arange(half, dtype=jnp.int32)
        offset = (which[:, None] - owners[None, :]) % half
        usable = offset < pairs
        first = jnp.minimum(2 * offset, S_DEV - 2)
        owner_grid = jnp.broadcast_to(owners[None, :], (half, RECS))
        station_a = orders[owner_grid, first]
        station_b = orders[owner_grid, first + 1]
        base = row * S_ROW + owner_grid * S_DEV
        entries = jnp.stack([base + station_a, base + station_b], axis=2).reshape(half, 2 * RECS)
        valid = jnp.stack([usable, usable], axis=2).reshape(half, 2 * RECS)
        position = jnp.arange(2 * RECS, dtype=jnp.int32)
        sort_key = jnp.where(valid, position[None, :], 2 * RECS + position[None, :])
        picked = jnp.argsort(sort_key, axis=1, stable=True)[:, :R_ST]
        lists = jnp.take_along_axis(entries, picked, axis=1)
        shuffle_keys = jax.random.split(jax.random.fold_in(row_key, 3), half)
        shuffles = jax.vmap(lambda k: jax.random.permutation(k, R_ST))(shuffle_keys)
        lists = jnp.take_along_axis(lists, shuffles, axis=1)
        filler = jax.random.randint(jax.random.fold_in(row_key, 4), (RECS, R_ST), 0, S, dtype=jnp.int32)
        table = filler.at[busy[:half]].set(lists)
        counts = jnp.zeros((RECS,), jnp.int32).at[busy[:half]].set(R_ST)
        return (table.reshape(RECS * R_ST), counts)
    tables, counts = jax.vmap(one_row)(jnp.arange(GRID_ROWS, dtype=jnp.int32))
    return (tables.reshape(SLOTS).astype(jnp.int32), counts.reshape(RECS * GRID_ROWS).astype(jnp.int32))


def draw_seg_count(key, part):
    return recorder_layout(key)[1]


def draw_slot_station(key, part):
    return recorder_layout(key)[0]


def draw_window_mask(key, part):
    start = jax.random.randint(jax.random.fold_in(key, 11), (S, 1), 0, W, dtype=jnp.int32)
    length = jax.random.randint(jax.random.fold_in(key, 12), (S, 1), 0, W + 1, dtype=jnp.int32)
    windows = jnp.arange(W, dtype=jnp.int32)[None, :]
    outage = (windows - start) % W < length
    return jnp.where(outage, 0, 1).astype(jnp.int32)


def steps_of(rng, dims, cuts, low, largest):
    gain, own = 1.0, jax.random.fold_in(rng, 6)
    for dim, parts in cuts:
        steps = jnp.exp(jax.random.uniform(jax.random.fold_in(own, dim), (parts,), jnp.float32, low / len(cuts), largest / len(cuts)))
        gain = gain * jnp.repeat(steps, dims[dim] // parts).reshape([-1 if axis == dim else 1 for axis in range(len(dims))])
    return gain


def normal_values(own_key, dims, spread, most, cuts=(), kind=jnp.bfloat16):
    result = spread * jax.random.normal(own_key, dims, jnp.float32)
    if cuts:
        result = result * steps_of(own_key, dims, cuts, -0.22, 0.18)
    return jnp.clip(result, -most, most).astype(kind)


def setup_inputs(seed: int = 0) -> dict:
    seeds = jax.random.split(jax.random.key(seed), 5)
    recorded = normal_values(seeds[0], (SLOTS, W, L), 1.0, 6.0, ((0, 32),))
    seg_count = draw_seg_count(jax.random.fold_in(seeds[4], 71), 0)
    slot_station = draw_slot_station(jax.random.fold_in(seeds[4], 71), 0)
    window_mask = draw_window_mask(jax.random.fold_in(seeds[4], 71), 0)
    return dict(recorded=recorded, seg_count=seg_count, slot_station=slot_station, window_mask=window_mask)


def transform_table():
    times = jnp.arange(L, dtype=jnp.int32)
    freqs = jnp.arange(F, dtype=jnp.int32) + F0
    phase = times[:, None] * freqs[None, :] % L
    angle = phase.astype(jnp.float32) * (2.0 * math.pi / L)
    return jnp.concatenate([jnp.cos(angle), -jnp.sin(angle)], axis=1).astype(jnp.bfloat16)

def whiten(segments, table):
    count = segments.shape[0]
    spectrum = jnp.dot(segments.reshape(count * W, L), table, preferred_element_type=jnp.float32)
    real = spectrum[:, :F]
    imag = spectrum[:, F:]
    power = (real * real + imag * imag).reshape(count * W, F // BAND, BAND)
    factor = lax.rsqrt(lax.optimization_barrier(jnp.mean(power, axis=2)) + 1e-05)
    factor = jnp.repeat(factor, BAND, axis=1)
    white = jnp.concatenate([real * factor, imag * factor], axis=1)
    return white.astype(jnp.bfloat16).reshape(count, W, 2 * F)

def reference(recorded, seg_count, slot_station, window_mask):
    table = transform_table()
    slot = jnp.arange(SLOTS, dtype=jnp.int32)
    live = slot % R_ST < seg_count[slot // R_ST]
    target = jnp.where(live, slot_station, S).astype(jnp.int32)
    source = jnp.zeros((S,), jnp.int32).at[target].set(slot, mode='drop')
    blocks = source.reshape(S // S_DEV, S_DEV)

    def one_block(index):
        return whiten(jnp.take(recorded, index, axis=0), table)
    spectra = lax.map(one_block, blocks).reshape(S, W, 2 * F)
    mask_float = window_mask.astype(jnp.bfloat16)
    spectra = spectra * mask_float[:, :, None]
    stacked = spectra.reshape(S, W, 2, F).transpose(3, 0, 2, 1).reshape(F, S, 2 * W)
    column = jnp.arange(S, dtype=jnp.int32)
    within = column % NCB
    order = ((within // S_DEV * RECS + column // NCB) * S_DEV + within % S_DEV).astype(jnp.int32)
    right = jnp.take(stacked, order, axis=1)
    right_mask = jnp.take(mask_float, order, axis=0)
    counts = jnp.dot(mask_float, right_mask.T, preferred_element_type=jnp.float32)
    inverse = 1.0 / jnp.maximum(counts, 1.0)
    swapped = jnp.concatenate([right[:, :, W:], -right[:, :, :W]], axis=2)

    def one_bin(group):
        left, plain, turned = group
        left = left.astype(jnp.float32)
        real = jnp.dot(left, plain.astype(jnp.float32).T)
        imag = jnp.dot(left, turned.astype(jnp.float32).T)
        return ((real * inverse).astype(jnp.bfloat16), (imag * inverse).astype(jnp.bfloat16))
    cross_real, cross_imag = lax.map(one_bin, (stacked, right, swapped))
    return (cross_real.transpose(1, 2, 0), cross_imag.transpose(1, 2, 0))
```

```python
import math

import jax
import jax.numpy as jnp
import numpy as np
from jax import lax
from jax.sharding import PartitionSpec as P

F = 384
L = 3072
F0 = 13
BAND = 64
CAP = 2
W = 64


def transform_table():
    times = np.arange(L, dtype=np.int64)
    freqs = np.arange(F, dtype=np.int64) + F0
    phase = times[:, None] * freqs[None, :] % L
    angle = phase.astype(np.float64) * (2.0 * math.pi / L)
    return np.concatenate([np.cos(angle), -np.sin(angle)], axis=1).astype(jnp.bfloat16)


def whiten(segments, table):
    count = segments.shape[0]
    spectrum = jnp.dot(segments.reshape(count * W, L), table, preferred_element_type=jnp.float32)
    real = spectrum[:, :F]
    imag = spectrum[:, F:]
    power = (real * real + imag * imag).reshape(count * W, F // BAND, BAND)
    factor = lax.rsqrt(jnp.mean(power, axis=2) + 1e-05)
    factor = jnp.repeat(factor, BAND, axis=1)
    white = jnp.concatenate([real * factor, imag * factor], axis=1)
    return white.astype(jnp.bfloat16).reshape(count, W, 2 * F)


def per_device(recorded, seg_count, slot_station, window_mask):
    columns = lax.axis_size("col")
    slots_here = recorded.shape[0]
    owned = window_mask.shape[0]
    outgoing = columns * CAP
    slot_index = jnp.arange(slots_here, dtype=jnp.int32)
    live = slot_index < seg_count[0]
    target_col = jnp.where(live, slot_station // owned % columns, columns)
    onehot = (target_col[:, None] == jnp.arange(columns, dtype=jnp.int32)[None, :]).astype(
        jnp.int32
    )
    earlier = jnp.cumsum(onehot, axis=0) - onehot
    rank = jnp.sum(earlier * onehot, axis=1)
    position = jnp.where(live, target_col * CAP + rank, outgoing)
    chosen = position[None, :] == jnp.arange(outgoing, dtype=jnp.int32)[:, None]
    source = jnp.sum(jnp.where(chosen, slot_index[None, :], 0), axis=1)
    local_id = jnp.sum(jnp.where(chosen, slot_station[None, :] % owned + 1, 0), axis=1) - 1
    labels = local_id.astype(jnp.bfloat16).reshape(columns, CAP)
    white = whiten(recorded, transform_table())
    payload = jnp.take(white, source, axis=0, mode="clip").reshape(columns, CAP, W, 2 * F)
    tags = lax.all_to_all(labels, "col", split_axis=0, concat_axis=0, tiled=True)
    arrived = lax.all_to_all(payload, "col", split_axis=0, concat_axis=0, tiled=True)
    tags = tags.reshape(outgoing).astype(jnp.int32)
    flat = arrived.reshape(outgoing, W, 2 * F)
    match = tags[None, :] == jnp.arange(owned, dtype=jnp.int32)[:, None]
    pick = jnp.sum(jnp.where(match, jnp.arange(outgoing, dtype=jnp.int32)[None, :], 0), axis=1)
    mask_float = window_mask.astype(jnp.bfloat16)
    spectra = jnp.take(flat, pick, axis=0, mode="clip") * mask_float[:, :, None]
    stacked = spectra.reshape(owned, W, 2, F).transpose(3, 0, 2, 1).reshape(F, owned, 2 * W)
    left, left_mask = (
        lax.all_gather(stacked, "col", axis=1, tiled=True),
        lax.all_gather(mask_float, "col", axis=0, tiled=True),
    )
    right, right_mask = (
        lax.all_gather(stacked, "row", axis=1, tiled=True),
        lax.all_gather(mask_float, "row", axis=0, tiled=True),
    )
    counts = jnp.dot(left_mask, right_mask.T, preferred_element_type=jnp.float32)
    inverse = 1.0 / jnp.maximum(counts, 1.0)
    across = right.shape[1]
    turned = jnp.concatenate([right[:, :, W:], -right[:, :, :W]], axis=2)
    both = jnp.concatenate([right, turned], axis=1)
    product = jnp.einsum("fiw,fjw->ijf", left, both, preferred_element_type=jnp.float32)
    real_part = (product[:, :across, :] * inverse[:, :, None]).astype(jnp.bfloat16)
    imag_part = (product[:, across:, :] * inverse[:, :, None]).astype(jnp.bfloat16)
    return (real_part, imag_part)


def solution(mesh):
    placed = (
        P(("row", "col"), None, None),
        P(("row", "col")),
        P(("row", "col")),
        P(("row", "col"), None),
    )
    return jax.shard_map(
        per_device,
        mesh=mesh,
        in_specs=placed,
        out_specs=(P("row", "col", None), P("row", "col", None)),
        check_vma=False,
    )
```

```python
import functools
import math

import jax
import jax.numpy as jnp
import numpy as np
from jax import lax
from jax.experimental import pallas as pl
from jax.experimental.pallas import tpu as pltpu
from jax.sharding import PartitionSpec as P

F = 384
L = 3072
F0 = 13
BAND = 64
CAP = 2
W = 64
CHUNK = 128
HEAD = 16
MESH = pl.DeviceIdType.MESH


def transform_table():
    times = np.arange(L, dtype=np.int64)
    freqs = np.arange(F, dtype=np.int64) + F0
    phase = times[:, None] * freqs[None, :] % L
    angle = phase.astype(np.float64) * (2.0 * math.pi / L)
    return np.concatenate([np.cos(angle), -np.sin(angle)], axis=1).astype(jnp.bfloat16)


def whiten(segments, table):
    count = segments.shape[0]
    spectrum = jnp.dot(segments.reshape(count * W, L), table, preferred_element_type=jnp.float32)
    real = spectrum[:, :F]
    imag = spectrum[:, F:]
    power = (real * real + imag * imag).reshape(count * W, F // BAND, BAND)
    factor = lax.rsqrt(jnp.mean(power, axis=2) + 1e-05)
    factor = jnp.repeat(factor, BAND, axis=1)
    white = jnp.concatenate([real * factor, imag * factor], axis=1)
    return white.astype(jnp.bfloat16).reshape(count, W, 2 * F)


def flipped(value, bit):
    return value + (1 << bit) * (1 - 2 * ((value // (1 << bit)) % 2))


def masked(value, mask):
    bit = 0
    while mask >> bit:
        if (mask >> bit) & 1:
            value = flipped(value, bit)
        bit += 1
    return value


def gather_kernel(
    rows, cols, owned, x_ref, head_ref, real_ref, imag_ref,
    left, right, turnpad, local_sem, cube_send, cube_recv, up_send, up_recv, down_send, down_recv,
):
    row = lax.axis_index("row")
    col = lax.axis_index("col")
    bits = cols.bit_length() - 1
    chunks = F // CHUNK
    depth = CHUNK * owned
    stations = cols * owned
    across = rows * owned
    orders = ([*range(1, bits), 0], [*range(2, bits), 1, 0])

    def span(chunk, half):
        first = HEAD + chunk * depth + half * (depth // 2)
        if half == 0 and chunk == 0:
            return pl.ds(0, HEAD + depth // 2)
        return pl.ds(first, depth // 2)

    def whole_span(chunk):
        if chunk == 0:
            return pl.ds(0, HEAD + depth)
        return pl.ds(HEAD + chunk * depth, depth)

    def cube_copies(chunk, stage):
        copies = []
        for half in range(2):
            order = orders[half]
            partner = flipped(col, order[stage])
            for member in range(1 << stage):
                mask = 0
                for place in range(stage):
                    if (member >> place) & 1:
                        mask |= 1 << order[place]
                block = masked(col, mask)
                index = (1 << stage) - 1 + member
                ref = left.at[block, span(chunk, half), :]
                copies.append(
                    pltpu.make_async_remote_copy(
                        src_ref=ref,
                        dst_ref=ref,
                        send_sem=cube_send.at[chunk, half, index],
                        recv_sem=cube_recv.at[chunk, half, index],
                        device_id=(row, partner),
                        device_id_type=MESH,
                    )
                )
        return copies

    def line_copy(chunk, stage, up):
        step = 1 if up else -1
        block = row - step * stage
        block = jnp.clip(block, 0, rows - 1)
        ref = right.at[block, whole_span(chunk), :]
        send, recv = (up_send, up_recv) if up else (down_send, down_recv)
        return pltpu.make_async_remote_copy(
            src_ref=ref,
            dst_ref=ref,
            send_sem=send.at[chunk, stage],
            recv_sem=recv.at[chunk, stage],
            device_id=(jnp.clip(row + step, 0, rows - 1), col),
            device_id_type=MESH,
        )

    def line_arrival(chunk, stage, up):
        step = 1 if up else -1
        block = jnp.clip(row - step * (stage + 1), 0, rows - 1)
        ref = right.at[block, whole_span(chunk), :]
        send, recv = (up_send, up_recv) if up else (down_send, down_recv)
        return pltpu.make_async_remote_copy(
            src_ref=ref,
            dst_ref=ref,
            send_sem=send.at[chunk, stage],
            recv_sem=recv.at[chunk, stage],
            device_id=(jnp.clip(row + step, 0, rows - 1), col),
            device_id_type=MESH,
        )

    def sends(stage, up):
        if up:
            return jnp.logical_and(row - stage >= 0, row + 1 < rows)
        return jnp.logical_and(row + stage < rows, row >= 1)

    def receives(stage, up):
        if up:
            return row - 1 - stage >= 0
        return row + 1 + stage < rows

    def start_cube(chunk, stage):
        for copy in cube_copies(chunk, stage):
            copy.start()

    def land_cube(chunk, stage):
        for copy in cube_copies(chunk, stage):
            copy.wait_recv()

    def start_line(chunk, stage):
        for up in (True, False):
            @pl.when(sends(stage, up))
            def _():
                line_copy(chunk, stage, up).start()

    def land_line(chunk, stage):
        for up in (True, False):
            @pl.when(receives(stage, up))
            def _():
                line_arrival(chunk, stage, up).wait_recv()

    own = []
    for place, (target, index) in enumerate(((left, col), (right, row))):
        own.append(
            pltpu.make_async_copy(head_ref, target.at[index, pl.ds(0, HEAD), :], local_sem.at[place, 0])
        )
        own.append(
            pltpu.make_async_copy(
                x_ref, target.at[index, pl.ds(HEAD, F * owned), :], local_sem.at[place, 1]
            )
        )
    for copy in own:
        copy.start()

    barrier = pltpu.get_barrier_semaphore()
    for bit in range(bits):
        pl.semaphore_signal(
            barrier, inc=1, device_id=(row, flipped(col, bit)), device_id_type=MESH
        )

    @pl.when(row + 1 < rows)
    def _():
        pl.semaphore_signal(barrier, inc=1, device_id=(row + 1, col), device_id_type=MESH)

    @pl.when(row >= 1)
    def _():
        pl.semaphore_signal(barrier, inc=1, device_id=(row - 1, col), device_id_type=MESH)

    inner = jnp.logical_and(row + 1 < rows, row >= 1)
    pl.semaphore_wait(barrier, bits + jnp.where(inner, 2, 1))

    for copy in own:
        copy.wait()

    lane = lax.broadcasted_iota(jnp.int32, (across, 2 * W), 1)
    sign = jnp.where(lane < W, 1.0, -1.0)

    def inverse_counts():
        left_mask = jnp.concatenate(
            [left[c, 0:HEAD, :].astype(jnp.float32)[:owned] for c in range(cols)], axis=0
        ).astype(jnp.bfloat16)
        right_mask = jnp.concatenate(
            [right[r, 0:HEAD, :].astype(jnp.float32)[:owned] for r in range(rows)] * 2, axis=0
        ).astype(jnp.bfloat16)
        counts = lax.dot_general(
            left_mask, right_mask, (((1,), (1,)), ((), ())), preferred_element_type=jnp.float32
        )
        return 1.0 / jnp.maximum(counts, 1.0)

    def compute(chunk):
        inverse = inverse_counts()
        first = HEAD + chunk * depth

        def pair(index, carry):
            at = pl.ds(pl.multiple_of(first + index * 2 * owned, 2 * owned), 2 * owned)
            lefts = [left[c, at, :].astype(jnp.float32) for c in range(cols)]
            rights = [right[r, at, :].astype(jnp.float32) for r in range(rows)]
            for which in range(2):
                rows_of = slice(which * owned, (which + 1) * owned)
                one = jnp.concatenate([v[rows_of] for v in lefts], axis=0).astype(jnp.bfloat16)
                plain = jnp.concatenate([v[rows_of] for v in rights], axis=0)
                turned = pltpu.roll(plain, W, 1) * sign
                both = jnp.concatenate([plain, turned], axis=0).astype(jnp.bfloat16)
                product = lax.dot_general(
                    one, both, (((1,), (1,)), ((), ())), preferred_element_type=jnp.float32
                )
                put = pl.multiple_of((index * 2 + which) * stations, stations)
                turnpad[pl.ds(put, stations), 0 : 2 * across] = product * inverse
            return carry

        lax.fori_loop(0, CHUNK // 2, pair, 0, unroll=2)

        def station(index, carry):
            block = turnpad[pl.ds(index, CHUNK, stride=stations), :]
            block = block.T
            lanes = pl.ds(chunk * CHUNK, CHUNK)
            real_ref[index, :, lanes] = block[0:across].astype(jnp.bfloat16)
            imag_ref[index, :, lanes] = block[across : 2 * across].astype(jnp.bfloat16)
            return carry

        lax.fori_loop(0, stations, station, 0, unroll=2)

    line_stages = rows - 1
    stages = max(bits, line_stages)
    for slot in range(chunks + stages):
        for stage in range(stages, -1, -1):
            chunk = slot - stage
            if chunk < 0 or chunk >= chunks:
                continue
            if 1 <= stage <= bits:
                land_cube(chunk, stage - 1)
            if stage < bits:
                start_cube(chunk, stage)
            if 1 <= stage <= line_stages:
                land_line(chunk, stage - 1)
            if stage < line_stages:
                start_line(chunk, stage)
        done = slot - stages
        if 0 <= done < chunks:
            compute(done)

    for chunk in range(chunks):
        for stage in range(bits):
            for copy in cube_copies(chunk, stage):
                copy.wait_send()
        for stage in range(line_stages):
            for up in (True, False):
                @pl.when(sends(stage, up))
                def _():
                    line_copy(chunk, stage, up).wait_send()


def cross_spectra(stacked, head, owned):
    rows = lax.axis_size("row")
    cols = lax.axis_size("col")
    stations = cols * owned
    across = rows * owned
    chunks = F // CHUNK
    shape = jax.ShapeDtypeStruct((stations, across, F), jnp.bfloat16)
    depth = HEAD + F * owned
    return pl.pallas_call(
        functools.partial(gather_kernel, rows, cols, owned),
        out_shape=(shape, shape),
        in_specs=[pl.BlockSpec(memory_space=pl.ANY)] * 2,
        out_specs=[pl.BlockSpec(memory_space=pltpu.VMEM)] * 2,
        scratch_shapes=[
            pltpu.VMEM((cols, depth, 2 * W), jnp.bfloat16),
            pltpu.VMEM((rows, depth, 2 * W), jnp.bfloat16),
            pltpu.VMEM((CHUNK * stations, 2 * W), jnp.float32),
            pltpu.SemaphoreType.DMA((2, 2)),
            pltpu.SemaphoreType.DMA((chunks, 2, cols - 1)),
            pltpu.SemaphoreType.DMA((chunks, 2, cols - 1)),
            pltpu.SemaphoreType.DMA((chunks, rows - 1)),
            pltpu.SemaphoreType.DMA((chunks, rows - 1)),
            pltpu.SemaphoreType.DMA((chunks, rows - 1)),
            pltpu.SemaphoreType.DMA((chunks, rows - 1)),
        ],
        compiler_params=pltpu.CompilerParams(
            collective_id=0, has_side_effects=True, vmem_limit_bytes=56 * 1024 * 1024
        ),
        cost_estimate=pl.CostEstimate(
            flops=4 * F * stations * across * 2 * W, bytes_accessed=20_000_000, transcendentals=0
        ),
    )(stacked, head)


def per_device(recorded, seg_count, slot_station, window_mask):
    columns = lax.axis_size("col")
    slots_here = recorded.shape[0]
    owned = window_mask.shape[0]
    outgoing = columns * CAP
    slot_index = jnp.arange(slots_here, dtype=jnp.int32)
    live = slot_index < seg_count[0]
    target_col = jnp.where(live, slot_station // owned % columns, columns)
    onehot = (target_col[:, None] == jnp.arange(columns, dtype=jnp.int32)[None, :]).astype(
        jnp.int32
    )
    earlier = jnp.cumsum(onehot, axis=0) - onehot
    rank = jnp.sum(earlier * onehot, axis=1)
    position = jnp.where(live, target_col * CAP + rank, outgoing)
    chosen = position[None, :] == jnp.arange(outgoing, dtype=jnp.int32)[:, None]
    source = jnp.sum(jnp.where(chosen, slot_index[None, :], 0), axis=1)
    local_id = jnp.sum(jnp.where(chosen, slot_station[None, :] % owned + 1, 0), axis=1) - 1
    labels = local_id.astype(jnp.bfloat16).reshape(columns, CAP)
    white = whiten(recorded, transform_table())
    payload = jnp.take(white, source, axis=0, mode="clip").reshape(columns, CAP, W, 2 * F)
    tags = lax.all_to_all(labels, "col", split_axis=0, concat_axis=0, tiled=True)
    arrived = lax.all_to_all(payload, "col", split_axis=0, concat_axis=0, tiled=True)
    tags = tags.reshape(outgoing).astype(jnp.int32)
    flat = arrived.reshape(outgoing, W, 2 * F)
    match = tags[None, :] == jnp.arange(owned, dtype=jnp.int32)[:, None]
    pick = jnp.sum(jnp.where(match, jnp.arange(outgoing, dtype=jnp.int32)[None, :], 0), axis=1)
    mask_float = window_mask.astype(jnp.bfloat16)
    spectra = jnp.take(flat, pick, axis=0, mode="clip") * mask_float[:, :, None]
    stacked = spectra.reshape(owned, W, 2, F).transpose(3, 0, 2, 1).reshape(F, owned, 2 * W)
    head = jnp.pad(mask_float, ((0, HEAD - owned), (0, W)))
    return cross_spectra(stacked.reshape(F * owned, 2 * W), head, owned)


def solution(mesh):
    placed = (
        P(("row", "col"), None, None),
        P(("row", "col")),
        P(("row", "col")),
        P(("row", "col"), None),
    )
    return jax.shard_map(
        per_device,
        mesh=mesh,
        in_specs=placed,
        out_specs=(P("row", "col", None), P("row", "col", None)),
        check_vma=False,
    )
```

```python
import functools
import math

import jax
import jax.numpy as jnp
import numpy as np
from jax import lax
from jax.experimental import pallas as pl
from jax.experimental.pallas import tpu as pltpu
from jax.sharding import PartitionSpec as P

F = 384
L = 3072
F0 = 13
BAND = 64
CAP = 2
W = 64
CHUNK = 128
HEAD = 16
GROUP = 8
BATCH = 4
MESH = pl.DeviceIdType.MESH


def transform_table():
    times = np.arange(L, dtype=np.int64)
    freqs = np.arange(F, dtype=np.int64) + F0
    phase = times[:, None] * freqs[None, :] % L
    angle = phase.astype(np.float64) * (2.0 * math.pi / L)
    return np.concatenate([np.cos(angle), -np.sin(angle)], axis=1).astype(jnp.bfloat16)


def band_means():
    band = np.arange(F) // BAND
    return ((band[:, None] == band[None, :]) / BAND).astype(jnp.bfloat16)


def whiten_kernel(source_ref, *refs):
    segments = jnp.concatenate([ref[0] for ref in refs[:BATCH]], axis=0)
    table_ref, band_ref, out_ref = refs[BATCH:]
    spectrum = jnp.dot(segments, table_ref[...], preferred_element_type=jnp.float32)
    real = spectrum[:, :F]
    imag = spectrum[:, F:]
    power = real * real + imag * imag
    high = power.astype(jnp.bfloat16)
    low = (power - high.astype(jnp.float32)).astype(jnp.bfloat16)
    band = band_ref[...]
    mean = jnp.dot(high, band, preferred_element_type=jnp.float32) + jnp.dot(
        low, band, preferred_element_type=jnp.float32
    )
    factor = lax.rsqrt(mean + 1e-05)
    white = jnp.concatenate([real * factor, imag * factor], axis=1)
    out_ref[...] = white.astype(jnp.bfloat16).reshape(BATCH, W, 2 * F)


def whiten(recorded, source):
    outgoing = source.shape[0]

    def picked(place):
        return pl.BlockSpec((1, W, L), lambda g, src: (src[g * BATCH + place], 0, 0))

    return pl.pallas_call(
        whiten_kernel,
        grid_spec=pltpu.PrefetchScalarGridSpec(
            num_scalar_prefetch=1,
            grid=(outgoing // BATCH,),
            in_specs=[picked(place) for place in range(BATCH)]
            + [
                pl.BlockSpec((L, 2 * F), lambda g, src: (0, 0)),
                pl.BlockSpec((F, F), lambda g, src: (0, 0)),
            ],
            out_specs=pl.BlockSpec((BATCH, W, 2 * F), lambda g, src: (g, 0, 0)),
        ),
        out_shape=jax.ShapeDtypeStruct((outgoing, W, 2 * F), jnp.bfloat16),
        compiler_params=pltpu.CompilerParams(vmem_limit_bytes=48 * 1024 * 1024),
    )(source, *[recorded] * BATCH, jnp.asarray(transform_table()), jnp.asarray(band_means()))


def flipped(value, bit):
    return value + (1 << bit) * (1 - 2 * ((value // (1 << bit)) % 2))


def masked(value, mask):
    bit = 0
    while mask >> bit:
        if (mask >> bit) & 1:
            value = flipped(value, bit)
        bit += 1
    return value


def gather_kernel(
    rows, cols, owned, x_ref, head_ref, real_ref, imag_ref,
    left, right, turnpad, local_sem, cube_send, cube_recv, up_send, up_recv, down_send, down_recv,
):
    row = lax.axis_index("row")
    col = lax.axis_index("col")
    bits = cols.bit_length() - 1
    chunks = F // CHUNK
    depth = CHUNK * owned
    stations = cols * owned
    across = rows * owned
    orders = ([*range(1, bits), 0], [*range(2, bits), 1, 0])

    def span(chunk, half):
        first = HEAD + chunk * depth + half * (depth // 2)
        if half == 0 and chunk == 0:
            return pl.ds(0, HEAD + depth // 2)
        return pl.ds(first, depth // 2)

    def whole_span(chunk):
        if chunk == 0:
            return pl.ds(0, HEAD + depth)
        return pl.ds(HEAD + chunk * depth, depth)

    def cube_copies(chunk, stage):
        copies = []
        for half in range(2):
            order = orders[half]
            partner = flipped(col, order[stage])
            for member in range(1 << stage):
                mask = 0
                for place in range(stage):
                    if (member >> place) & 1:
                        mask |= 1 << order[place]
                block = masked(col, mask)
                index = (1 << stage) - 1 + member
                ref = left.at[block, span(chunk, half), :]
                copies.append(
                    pltpu.make_async_remote_copy(
                        src_ref=ref,
                        dst_ref=ref,
                        send_sem=cube_send.at[chunk, half, index],
                        recv_sem=cube_recv.at[chunk, half, index],
                        device_id=(row, partner),
                        device_id_type=MESH,
                    )
                )
        return copies

    def line_copy(chunk, stage, up):
        step = 1 if up else -1
        block = row - step * stage
        block = jnp.clip(block, 0, rows - 1)
        ref = right.at[block, whole_span(chunk), :]
        send, recv = (up_send, up_recv) if up else (down_send, down_recv)
        return pltpu.make_async_remote_copy(
            src_ref=ref,
            dst_ref=ref,
            send_sem=send.at[chunk, stage],
            recv_sem=recv.at[chunk, stage],
            device_id=(jnp.clip(row + step, 0, rows - 1), col),
            device_id_type=MESH,
        )

    def line_arrival(chunk, stage, up):
        step = 1 if up else -1
        block = jnp.clip(row - step * (stage + 1), 0, rows - 1)
        ref = right.at[block, whole_span(chunk), :]
        send, recv = (up_send, up_recv) if up else (down_send, down_recv)
        return pltpu.make_async_remote_copy(
            src_ref=ref,
            dst_ref=ref,
            send_sem=send.at[chunk, stage],
            recv_sem=recv.at[chunk, stage],
            device_id=(jnp.clip(row + step, 0, rows - 1), col),
            device_id_type=MESH,
        )

    def sends(stage, up):
        if up:
            return jnp.logical_and(row - stage >= 0, row + 1 < rows)
        return jnp.logical_and(row + stage < rows, row >= 1)

    def receives(stage, up):
        if up:
            return row - 1 - stage >= 0
        return row + 1 + stage < rows

    def start_cube(chunk, stage):
        for copy in cube_copies(chunk, stage):
            copy.start()

    def land_cube(chunk, stage):
        for copy in cube_copies(chunk, stage):
            copy.wait_recv()

    def start_line(chunk, stage):
        for up in (True, False):
            @pl.when(sends(stage, up))
            def _():
                line_copy(chunk, stage, up).start()

    def land_line(chunk, stage):
        for up in (True, False):
            @pl.when(receives(stage, up))
            def _():
                line_arrival(chunk, stage, up).wait_recv()

    own = []
    for place, (target, index) in enumerate(((left, col), (right, row))):
        own.append(
            pltpu.make_async_copy(head_ref, target.at[index, pl.ds(0, HEAD), :], local_sem.at[place, 0])
        )
        own.append(
            pltpu.make_async_copy(
                x_ref, target.at[index, pl.ds(HEAD, F * owned), :], local_sem.at[place, 1]
            )
        )
    for copy in own:
        copy.start()

    barrier = pltpu.get_barrier_semaphore()
    for bit in range(bits):
        pl.semaphore_signal(
            barrier, inc=1, device_id=(row, flipped(col, bit)), device_id_type=MESH
        )

    @pl.when(row + 1 < rows)
    def _():
        pl.semaphore_signal(barrier, inc=1, device_id=(row + 1, col), device_id_type=MESH)

    @pl.when(row >= 1)
    def _():
        pl.semaphore_signal(barrier, inc=1, device_id=(row - 1, col), device_id_type=MESH)

    inner = jnp.logical_and(row + 1 < rows, row >= 1)
    pl.semaphore_wait(barrier, bits + jnp.where(inner, 2, 1))

    for copy in own:
        copy.wait()

    lane = lax.broadcasted_iota(jnp.int32, (across, 2 * W), 1)
    sign = jnp.where(lane < W, 1.0, -1.0)
    empty = jnp.zeros((2 * across, 2 * W), jnp.bfloat16)
    half_cols = cols // 2
    half_stations = stations // 2
    planes = 4 * across // 128

    def paired(lefts, both):
        low = jnp.concatenate(lefts[:half_cols], axis=0)
        high = jnp.concatenate(lefts[half_cols:], axis=0)
        one = jnp.concatenate([low, high], axis=1).astype(jnp.bfloat16)
        both = both.astype(jnp.bfloat16)
        wide = jnp.concatenate(
            [
                jnp.concatenate([both, empty], axis=1),
                jnp.concatenate([empty, both], axis=1),
            ],
            axis=0,
        )
        return lax.dot_general(
            one, wide, (((1,), (1,)), ((), ())), preferred_element_type=jnp.float32
        )

    def inverse_counts():
        lefts = [left[c, 0:HEAD, :].astype(jnp.float32)[:owned] for c in range(cols)]
        rights = [right[r, 0:HEAD, :].astype(jnp.float32)[:owned] for r in range(rows)]
        counts = paired(lefts, jnp.concatenate(rights * 2, axis=0))
        return 1.0 / jnp.maximum(counts, 1.0)

    def compute(chunk):
        inverse = inverse_counts()
        first = HEAD + chunk * depth

        def group(index, carry):
            at = pl.ds(pl.multiple_of(first + index * GROUP * owned, GROUP * owned // 4), GROUP * owned)
            lefts = [left[c, at, :].astype(jnp.float32) for c in range(cols)]
            rights = [right[r, at, :].astype(jnp.float32) for r in range(rows)]
            for which in range(GROUP):
                rows_of = slice(which * owned, (which + 1) * owned)
                plain = jnp.concatenate([v[rows_of] for v in rights], axis=0)
                turned = pltpu.roll(plain, W, 1) * sign
                product = paired(
                    [v[rows_of] for v in lefts], jnp.concatenate([plain, turned], axis=0)
                )
                put = pl.multiple_of((index * GROUP + which) * half_stations, half_stations)
                scaled = product * inverse
                for plane in range(planes):
                    turnpad[plane, pl.ds(put, half_stations), :] = scaled[
                        :, plane * 128 : (plane + 1) * 128
                    ]
            return carry

        lax.fori_loop(0, CHUNK // GROUP, group, 0)

        def station(index, carry):
            block = jnp.concatenate(
                [
                    turnpad[plane, pl.ds(index, CHUNK, stride=half_stations), :].T
                    for plane in range(planes)
                ],
                axis=0,
            )
            lanes = pl.ds(chunk * CHUNK, CHUNK)
            for half in range(2):
                base = half * 2 * across
                put = index + half * half_stations
                real_ref[put, :, lanes] = block[base : base + across].astype(jnp.bfloat16)
                imag_ref[put, :, lanes] = block[base + across : base + 2 * across].astype(
                    jnp.bfloat16
                )
            return carry

        lax.fori_loop(0, half_stations, station, 0, unroll=4)

    line_stages = rows - 1
    stages = max(bits, line_stages)
    for slot in range(chunks + stages):
        for stage in range(stages, -1, -1):
            chunk = slot - stage
            if chunk < 0 or chunk >= chunks:
                continue
            if 1 <= stage <= bits:
                land_cube(chunk, stage - 1)
            if stage < bits:
                start_cube(chunk, stage)
            if 1 <= stage <= line_stages:
                land_line(chunk, stage - 1)
            if stage < line_stages:
                start_line(chunk, stage)
        done = slot - stages
        if 0 <= done < chunks:
            compute(done)

    for chunk in range(chunks):
        for stage in range(bits):
            for copy in cube_copies(chunk, stage):
                copy.wait_send()
        for stage in range(line_stages):
            for up in (True, False):
                @pl.when(sends(stage, up))
                def _():
                    line_copy(chunk, stage, up).wait_send()


def cross_spectra(stacked, head, owned):
    rows = lax.axis_size("row")
    cols = lax.axis_size("col")
    stations = cols * owned
    across = rows * owned
    chunks = F // CHUNK
    shape = jax.ShapeDtypeStruct((stations, across, F), jnp.bfloat16)
    depth = HEAD + F * owned
    return pl.pallas_call(
        functools.partial(gather_kernel, rows, cols, owned),
        out_shape=(shape, shape),
        in_specs=[pl.BlockSpec(memory_space=pl.ANY)] * 2,
        out_specs=[pl.BlockSpec(memory_space=pltpu.VMEM)] * 2,
        scratch_shapes=[
            pltpu.VMEM((cols, depth, 2 * W), jnp.bfloat16),
            pltpu.VMEM((rows, depth, 2 * W), jnp.bfloat16),
            pltpu.VMEM((4 * across // 128, CHUNK * stations // 2, 128), jnp.float32),
            pltpu.SemaphoreType.DMA((2, 2)),
            pltpu.SemaphoreType.DMA((chunks, 2, cols - 1)),
            pltpu.SemaphoreType.DMA((chunks, 2, cols - 1)),
            pltpu.SemaphoreType.DMA((chunks, rows - 1)),
            pltpu.SemaphoreType.DMA((chunks, rows - 1)),
            pltpu.SemaphoreType.DMA((chunks, rows - 1)),
            pltpu.SemaphoreType.DMA((chunks, rows - 1)),
        ],
        compiler_params=pltpu.CompilerParams(
            collective_id=0, has_side_effects=True, vmem_limit_bytes=56 * 1024 * 1024
        ),
        cost_estimate=pl.CostEstimate(
            flops=4 * F * stations * across * 2 * W, bytes_accessed=20_000_000, transcendentals=0
        ),
    )(stacked, head)


def per_device(recorded, seg_count, slot_station, window_mask):
    columns = lax.axis_size("col")
    slots_here = recorded.shape[0]
    owned = window_mask.shape[0]
    outgoing = columns * CAP
    slot_index = jnp.arange(slots_here, dtype=jnp.int32)
    live = slot_index < seg_count[0]
    target_col = jnp.where(live, slot_station // owned % columns, columns)
    onehot = (target_col[:, None] == jnp.arange(columns, dtype=jnp.int32)[None, :]).astype(
        jnp.int32
    )
    earlier = jnp.cumsum(onehot, axis=0) - onehot
    rank = jnp.sum(earlier * onehot, axis=1)
    position = jnp.where(live, target_col * CAP + rank, outgoing)
    chosen = position[None, :] == jnp.arange(outgoing, dtype=jnp.int32)[:, None]
    source = jnp.sum(jnp.where(chosen, slot_index[None, :], 0), axis=1)
    local_id = jnp.sum(jnp.where(chosen, slot_station[None, :] % owned + 1, 0), axis=1) - 1
    labels = local_id.astype(jnp.bfloat16).reshape(columns, CAP)
    white = whiten(recorded, source.astype(jnp.int32))
    payload = white.reshape(columns, CAP, W, 2 * F)
    tags = lax.all_to_all(labels, "col", split_axis=0, concat_axis=0, tiled=True)
    arrived = lax.all_to_all(payload, "col", split_axis=0, concat_axis=0, tiled=True)
    tags = tags.reshape(outgoing).astype(jnp.int32)
    flat = arrived.reshape(outgoing, W, 2 * F)
    match = tags[None, :] == jnp.arange(owned, dtype=jnp.int32)[:, None]
    pick = jnp.sum(jnp.where(match, jnp.arange(outgoing, dtype=jnp.int32)[None, :], 0), axis=1)
    mask_float = window_mask.astype(jnp.bfloat16)
    spectra = jnp.take(flat, pick, axis=0, mode="clip") * mask_float[:, :, None]
    stacked = spectra.reshape(owned, W, 2, F).transpose(3, 0, 2, 1).reshape(F, owned, 2 * W)
    head = jnp.pad(mask_float, ((0, HEAD - owned), (0, W)))
    return cross_spectra(stacked.reshape(F * owned, 2 * W), head, owned)


def solution(mesh):
    placed = (
        P(("row", "col"), None, None),
        P(("row", "col")),
        P(("row", "col")),
        P(("row", "col"), None),
    )
    return jax.shard_map(
        per_device,
        mesh=mesh,
        in_specs=placed,
        out_specs=(P("row", "col", None), P("row", "col", None)),
        check_vma=False,
    )
```

```python
import functools
import math

import jax
import jax.numpy as jnp
import numpy as np
from jax import lax
from jax.experimental import pallas as pl
from jax.experimental.pallas import tpu as pltpu
from jax.sharding import PartitionSpec as P

F = 384
L = 3072
F0 = 13
BAND = 64
CAP = 2
W = 64
CHUNK = 128
HEAD = 16
GROUP = 8
BATCH = 4
MESH = pl.DeviceIdType.MESH


def transform_table():
    times = np.arange(L, dtype=np.int64)
    freqs = np.arange(F, dtype=np.int64) + F0
    phase = times[:, None] * freqs[None, :] % L
    angle = phase.astype(np.float64) * (2.0 * math.pi / L)
    return np.concatenate([np.cos(angle), -np.sin(angle)], axis=1).astype(jnp.bfloat16)


def band_means():
    band = np.arange(F) // BAND
    return ((band[:, None] == band[None, :]) / BAND).astype(jnp.bfloat16)


def whiten_kernel(source_ref, *refs):
    segments = jnp.concatenate([ref[0] for ref in refs[:BATCH]], axis=0)
    table_ref, band_ref, out_ref = refs[BATCH:]
    spectrum = jnp.dot(segments, table_ref[...], preferred_element_type=jnp.float32)
    real = spectrum[:, :F]
    imag = spectrum[:, F:]
    power = real * real + imag * imag
    high = power.astype(jnp.bfloat16)
    low = (power - high.astype(jnp.float32)).astype(jnp.bfloat16)
    band = band_ref[...]
    mean = jnp.dot(high, band, preferred_element_type=jnp.float32) + jnp.dot(
        low, band, preferred_element_type=jnp.float32
    )
    factor = lax.rsqrt(mean + 1e-05)
    real = real * factor
    imag = imag * factor
    for chunk in range(F // CHUNK):
        lanes = slice(chunk * CHUNK, (chunk + 1) * CHUNK)
        white = jnp.concatenate([real[:, lanes], imag[:, lanes]], axis=1)
        out_ref[chunk] = white.astype(jnp.bfloat16).reshape(BATCH, W, 2 * CHUNK)


def whiten(recorded, source):
    outgoing = source.shape[0]

    def picked(place):
        return pl.BlockSpec((1, W, L), lambda g, src: (src[g * BATCH + place], 0, 0))

    return pl.pallas_call(
        whiten_kernel,
        grid_spec=pltpu.PrefetchScalarGridSpec(
            num_scalar_prefetch=1,
            grid=(outgoing // BATCH,),
            in_specs=[picked(place) for place in range(BATCH)]
            + [
                pl.BlockSpec((L, 2 * F), lambda g, src: (0, 0)),
                pl.BlockSpec((F, F), lambda g, src: (0, 0)),
            ],
            out_specs=pl.BlockSpec(
                (F // CHUNK, BATCH, W, 2 * CHUNK), lambda g, src: (0, g, 0, 0)
            ),
        ),
        out_shape=jax.ShapeDtypeStruct((F // CHUNK, outgoing, W, 2 * CHUNK), jnp.bfloat16),
        compiler_params=pltpu.CompilerParams(vmem_limit_bytes=48 * 1024 * 1024),
    )(source, *[recorded] * BATCH, jnp.asarray(transform_table()), jnp.asarray(band_means()))


def flipped(value, bit):
    return value + (1 << bit) * (1 - 2 * ((value // (1 << bit)) % 2))


def masked(value, mask):
    bit = 0
    while mask >> bit:
        if (mask >> bit) & 1:
            value = flipped(value, bit)
        bit += 1
    return value


def gather_kernel(
    rows, cols, owned, white_ref, tag_ref, head_ref, mask_ref, real_ref, imag_ref,
    left, right, turnpad, arrived, tags, mixed, local_sem, swap_send, swap_recv, tag_send, tag_recv, cube_send, cube_recv, up_send, up_recv, down_send, down_recv,
):
    row = lax.axis_index("row")
    col = lax.axis_index("col")
    bits = cols.bit_length() - 1
    chunks = F // CHUNK
    depth = CHUNK * owned
    stations = cols * owned
    across = rows * owned
    orders = ([*range(1, bits), 0], [*range(2, bits), 1, 0])

    def span(chunk, half):
        first = HEAD + chunk * depth + half * (depth // 2)
        if half == 0 and chunk == 0:
            return pl.ds(0, HEAD + depth // 2)
        return pl.ds(first, depth // 2)

    def whole_span(chunk):
        if chunk == 0:
            return pl.ds(0, HEAD + depth)
        return pl.ds(HEAD + chunk * depth, depth)

    def cube_copies(chunk, stage):
        copies = []
        for half in range(2):
            order = orders[half]
            partner = flipped(col, order[stage])
            for member in range(1 << stage):
                mask = 0
                for place in range(stage):
                    if (member >> place) & 1:
                        mask |= 1 << order[place]
                block = masked(col, mask)
                index = (1 << stage) - 1 + member
                ref = left.at[block, span(chunk, half), :]
                copies.append(
                    pltpu.make_async_remote_copy(
                        src_ref=ref,
                        dst_ref=ref,
                        send_sem=cube_send.at[chunk, half, index],
                        recv_sem=cube_recv.at[chunk, half, index],
                        device_id=(row, partner),
                        device_id_type=MESH,
                    )
                )
        return copies

    def line_copy(chunk, stage, up):
        step = 1 if up else -1
        block = row - step * stage
        block = jnp.clip(block, 0, rows - 1)
        ref = right.at[block, whole_span(chunk), :]
        send, recv = (up_send, up_recv) if up else (down_send, down_recv)
        return pltpu.make_async_remote_copy(
            src_ref=ref,
            dst_ref=ref,
            send_sem=send.at[chunk, stage],
            recv_sem=recv.at[chunk, stage],
            device_id=(jnp.clip(row + step, 0, rows - 1), col),
            device_id_type=MESH,
        )

    def line_arrival(chunk, stage, up):
        step = 1 if up else -1
        block = jnp.clip(row - step * (stage + 1), 0, rows - 1)
        ref = right.at[block, whole_span(chunk), :]
        send, recv = (up_send, up_recv) if up else (down_send, down_recv)
        return pltpu.make_async_remote_copy(
            src_ref=ref,
            dst_ref=ref,
            send_sem=send.at[chunk, stage],
            recv_sem=recv.at[chunk, stage],
            device_id=(jnp.clip(row + step, 0, rows - 1), col),
            device_id_type=MESH,
        )

    def sends(stage, up):
        if up:
            return jnp.logical_and(row - stage >= 0, row + 1 < rows)
        return jnp.logical_and(row + stage < rows, row >= 1)

    def receives(stage, up):
        if up:
            return row - 1 - stage >= 0
        return row + 1 + stage < rows

    def start_cube(chunk, stage):
        for copy in cube_copies(chunk, stage):
            copy.start()

    def land_cube(chunk, stage):
        for copy in cube_copies(chunk, stage):
            copy.wait_recv()

    def start_line(chunk, stage):
        for up in (True, False):
            @pl.when(sends(stage, up))
            def _():
                line_copy(chunk, stage, up).start()

    def land_line(chunk, stage):
        for up in (True, False):
            @pl.when(receives(stage, up))
            def _():
                line_arrival(chunk, stage, up).wait_recv()

    own = []
    for place, (target, index) in enumerate(((left, col), (right, row))):
        own.append(
            pltpu.make_async_copy(head_ref, target.at[index, pl.ds(0, HEAD), :], local_sem.at[place, 0])
        )
    for chunk in range(chunks):
        own.append(
            pltpu.make_async_copy(
                white_ref.at[chunk, col], arrived.at[chunk, col], local_sem.at[2, chunk]
            )
        )
    own.append(pltpu.make_async_copy(tag_ref.at[col], tags.at[col], local_sem.at[0, 1]))
    for copy in own:
        copy.start()

    barrier = pltpu.get_barrier_semaphore()
    for member in range(1, cols):
        pl.semaphore_signal(
            barrier, inc=1, device_id=(row, masked(col, member)), device_id_type=MESH
        )

    @pl.when(row + 1 < rows)
    def _():
        pl.semaphore_signal(barrier, inc=1, device_id=(row + 1, col), device_id_type=MESH)

    @pl.when(row >= 1)
    def _():
        pl.semaphore_signal(barrier, inc=1, device_id=(row - 1, col), device_id_type=MESH)

    inner = jnp.logical_and(row + 1 < rows, row >= 1)
    pl.semaphore_wait(barrier, cols - 1 + jnp.where(inner, 2, 1))

    def tag_copy(member, landing):
        partner = masked(col, member)
        return pltpu.make_async_remote_copy(
            src_ref=tag_ref.at[partner],
            dst_ref=tags.at[partner if landing else col],
            send_sem=tag_send.at[member - 1],
            recv_sem=tag_recv.at[member - 1],
            device_id=(row, partner),
            device_id_type=MESH,
        )

    def swap_copy(chunk, member, landing):
        partner = masked(col, member)
        return pltpu.make_async_remote_copy(
            src_ref=white_ref.at[chunk, partner],
            dst_ref=arrived.at[chunk, partner if landing else col],
            send_sem=swap_send.at[chunk, member - 1],
            recv_sem=swap_recv.at[chunk, member - 1],
            device_id=(row, partner),
            device_id_type=MESH,
        )

    for member in range(1, cols):
        tag_copy(member, False).start()
    for chunk in range(chunks):
        for member in range(1, cols):
            swap_copy(chunk, member, False).start()
    for copy in own:
        copy.wait()

    def prepare(chunk):
        for member in range(1, cols):
            if chunk == 0:
                tag_copy(member, True).wait_recv()
            swap_copy(chunk, member, True).wait_recv()
        names = [tags[c].astype(jnp.float32) for c in range(cols)]
        names = [names[c][rank : rank + 1, :] for c in range(cols) for rank in range(CAP)]

        def choose(station, carry):
            name = station.astype(jnp.float32)
            total = jnp.zeros((W, 2 * CHUNK), jnp.float32)
            for slot in range(cols * CAP):
                weight = jnp.where(names[slot] == name, 1.0, 0.0)
                weight = jnp.concatenate([weight, weight], axis=1)
                total += arrived[chunk, slot // CAP, slot % CAP].astype(jnp.float32) * weight
            both = jnp.concatenate([total[:, :CHUNK], total[:, CHUNK:]], axis=0)
            mixed[pl.ds(station, CHUNK, stride=owned), :] = both.T * mask_ref[pl.ds(station, 1), :]
            return carry

        lax.fori_loop(0, owned, choose, 0)
        block = mixed[...].astype(jnp.bfloat16)
        at = pl.ds(HEAD + chunk * depth, depth)
        left[col, at, :] = block
        right[row, at, :] = block

    lane = lax.broadcasted_iota(jnp.int32, (across, 2 * W), 1)
    sign = jnp.where(lane < W, 1.0, -1.0)
    empty = jnp.zeros((2 * across, 2 * W), jnp.bfloat16)
    half_cols = cols // 2
    half_stations = stations // 2
    planes = 4 * across // 128

    def paired(lefts, both):
        low = jnp.concatenate(lefts[:half_cols], axis=0)
        high = jnp.concatenate(lefts[half_cols:], axis=0)
        one = jnp.concatenate([low, high], axis=1).astype(jnp.bfloat16)
        both = both.astype(jnp.bfloat16)
        wide = jnp.concatenate(
            [
                jnp.concatenate([both, empty], axis=1),
                jnp.concatenate([empty, both], axis=1),
            ],
            axis=0,
        )
        return lax.dot_general(
            one, wide, (((1,), (1,)), ((), ())), preferred_element_type=jnp.float32
        )

    def inverse_counts():
        lefts = [left[c, 0:HEAD, :].astype(jnp.float32)[:owned] for c in range(cols)]
        rights = [right[r, 0:HEAD, :].astype(jnp.float32)[:owned] for r in range(rows)]
        counts = paired(lefts, jnp.concatenate(rights * 2, axis=0))
        return 1.0 / jnp.maximum(counts, 1.0)

    def compute(chunk):
        inverse = inverse_counts()
        first = HEAD + chunk * depth

        def group(index, carry):
            at = pl.ds(pl.multiple_of(first + index * GROUP * owned, GROUP * owned // 4), GROUP * owned)
            lefts = [left[c, at, :].astype(jnp.float32) for c in range(cols)]
            rights = [right[r, at, :].astype(jnp.float32) for r in range(rows)]
            for which in range(GROUP):
                rows_of = slice(which * owned, (which + 1) * owned)
                plain = jnp.concatenate([v[rows_of] for v in rights], axis=0)
                turned = pltpu.roll(plain, W, 1) * sign
                product = paired(
                    [v[rows_of] for v in lefts], jnp.concatenate([plain, turned], axis=0)
                )
                put = pl.multiple_of((index * GROUP + which) * half_stations, half_stations)
                scaled = product * inverse
                for plane in range(planes):
                    turnpad[plane, pl.ds(put, half_stations), :] = scaled[
                        :, plane * 128 : (plane + 1) * 128
                    ]
            return carry

        lax.fori_loop(0, CHUNK // GROUP, group, 0)

        def station(index, carry):
            block = jnp.concatenate(
                [
                    turnpad[plane, pl.ds(index, CHUNK, stride=half_stations), :].T
                    for plane in range(planes)
                ],
                axis=0,
            )
            lanes = pl.ds(chunk * CHUNK, CHUNK)
            for half in range(2):
                base = half * 2 * across
                put = index + half * half_stations
                real_ref[put, :, lanes] = block[base : base + across].astype(jnp.bfloat16)
                imag_ref[put, :, lanes] = block[base + across : base + 2 * across].astype(
                    jnp.bfloat16
                )
            return carry

        lax.fori_loop(0, half_stations, station, 0, unroll=4)

    line_stages = rows - 1
    stages = max(bits, line_stages)
    for slot in range(chunks + stages):
        for stage in range(stages, -1, -1):
            chunk = slot - stage
            if chunk < 0 or chunk >= chunks:
                continue
            if 1 <= stage <= bits:
                land_cube(chunk, stage - 1)
            if stage == 0:
                prepare(chunk)
            if stage < bits:
                start_cube(chunk, stage)
            if 1 <= stage <= line_stages:
                land_line(chunk, stage - 1)
            if stage < line_stages:
                start_line(chunk, stage)
        done = slot - stages
        if 0 <= done < chunks:
            compute(done)

    for member in range(1, cols):
        tag_copy(member, False).wait_send()
        for chunk in range(chunks):
            swap_copy(chunk, member, False).wait_send()
    for chunk in range(chunks):
        for stage in range(bits):
            for copy in cube_copies(chunk, stage):
                copy.wait_send()
        for stage in range(line_stages):
            for up in (True, False):
                @pl.when(sends(stage, up))
                def _():
                    line_copy(chunk, stage, up).wait_send()


def cross_spectra(white, tags, head, mask, owned):
    rows = lax.axis_size("row")
    cols = lax.axis_size("col")
    stations = cols * owned
    across = rows * owned
    chunks = F // CHUNK
    shape = jax.ShapeDtypeStruct((stations, across, F), jnp.bfloat16)
    depth = HEAD + F * owned
    return pl.pallas_call(
        functools.partial(gather_kernel, rows, cols, owned),
        out_shape=(shape, shape),
        in_specs=[pl.BlockSpec(memory_space=pl.ANY)] * 3
        + [pl.BlockSpec(memory_space=pltpu.VMEM)],
        out_specs=[pl.BlockSpec(memory_space=pltpu.VMEM)] * 2,
        scratch_shapes=[
            pltpu.VMEM((cols, depth, 2 * W), jnp.bfloat16),
            pltpu.VMEM((rows, depth, 2 * W), jnp.bfloat16),
            pltpu.VMEM((4 * across // 128, CHUNK * stations // 2, 128), jnp.float32),
            pltpu.VMEM((chunks, cols, CAP, W, 2 * CHUNK), jnp.bfloat16),
            pltpu.VMEM((cols, HEAD, 2 * W), jnp.bfloat16),
            pltpu.VMEM((CHUNK * owned, 2 * W), jnp.float32),
            pltpu.SemaphoreType.DMA((3, max(chunks, 2))),
            pltpu.SemaphoreType.DMA((chunks, cols - 1)),
            pltpu.SemaphoreType.DMA((chunks, cols - 1)),
            pltpu.SemaphoreType.DMA((cols - 1,)),
            pltpu.SemaphoreType.DMA((cols - 1,)),
            pltpu.SemaphoreType.DMA((chunks, 2, cols - 1)),
            pltpu.SemaphoreType.DMA((chunks, 2, cols - 1)),
            pltpu.SemaphoreType.DMA((chunks, rows - 1)),
            pltpu.SemaphoreType.DMA((chunks, rows - 1)),
            pltpu.SemaphoreType.DMA((chunks, rows - 1)),
            pltpu.SemaphoreType.DMA((chunks, rows - 1)),
        ],
        compiler_params=pltpu.CompilerParams(
            collective_id=0, has_side_effects=True, vmem_limit_bytes=56 * 1024 * 1024
        ),
        cost_estimate=pl.CostEstimate(
            flops=4 * F * stations * across * 2 * W, bytes_accessed=20_000_000, transcendentals=0
        ),
    )(white, tags, head, mask)


def per_device(recorded, seg_count, slot_station, window_mask):
    columns = lax.axis_size("col")
    slots_here = recorded.shape[0]
    owned = window_mask.shape[0]
    outgoing = columns * CAP
    slot_index = jnp.arange(slots_here, dtype=jnp.int32)
    live = slot_index < seg_count[0]
    target_col = jnp.where(live, slot_station // owned % columns, columns)
    onehot = (target_col[:, None] == jnp.arange(columns, dtype=jnp.int32)[None, :]).astype(
        jnp.int32
    )
    earlier = jnp.cumsum(onehot, axis=0) - onehot
    rank = jnp.sum(earlier * onehot, axis=1)
    position = jnp.where(live, target_col * CAP + rank, outgoing)
    chosen = position[None, :] == jnp.arange(outgoing, dtype=jnp.int32)[:, None]
    source = jnp.sum(jnp.where(chosen, slot_index[None, :], 0), axis=1)
    local_id = jnp.sum(jnp.where(chosen, slot_station[None, :] % owned + 1, 0), axis=1) - 1
    labels = local_id.astype(jnp.bfloat16).reshape(columns, CAP, 1)
    labels = jnp.broadcast_to(jnp.pad(labels, ((0, 0), (0, HEAD - CAP), (0, 0))), (columns, HEAD, 2 * W))
    white = whiten(recorded, source.astype(jnp.int32))
    white = white.reshape(F // CHUNK, columns, CAP, W, 2 * CHUNK)
    mask_float = window_mask.astype(jnp.bfloat16)
    head = jnp.pad(mask_float, ((0, HEAD - owned), (0, W)))
    mask = jnp.concatenate([window_mask, window_mask], axis=1).astype(jnp.float32)
    return cross_spectra(white, labels, head, mask, owned)


def solution(mesh):
    placed = (
        P(("row", "col"), None, None),
        P(("row", "col")),
        P(("row", "col")),
        P(("row", "col"), None),
    )
    return jax.shard_map(
        per_device,
        mesh=mesh,
        in_specs=placed,
        out_specs=(P("row", "col", None), P("row", "col", None)),
        check_vma=False,
    )
```

```python
import functools
import math

import jax
import jax.numpy as jnp
import numpy as np
from jax import lax
from jax.experimental import pallas as pl
from jax.experimental.pallas import tpu as pltpu
from jax.sharding import PartitionSpec as P

F = 384
L = 3072
F0 = 13
BAND = 64
CAP = 2
W = 64
CHUNK = 128
HEAD = 16
GROUP = 8
BATCH = 8
MESH = pl.DeviceIdType.MESH


def transform_table():
    times = np.arange(L, dtype=np.int64)
    freqs = np.arange(F, dtype=np.int64) + F0
    phase = times[:, None] * freqs[None, :] % L
    angle = phase.astype(np.float64) * (2.0 * math.pi / L)
    return np.concatenate([np.cos(angle), -np.sin(angle)], axis=1).astype(jnp.bfloat16)


def band_means():
    band = np.arange(F) // BAND
    return ((band[:, None] == band[None, :]) / BAND).astype(jnp.bfloat16)


def whiten_kernel(source_ref, *refs):
    segments = jnp.concatenate([ref[0] for ref in refs[:BATCH]], axis=0)
    table_ref, band_ref, out_ref = refs[BATCH:]
    spectrum = jnp.dot(segments, table_ref[...], preferred_element_type=jnp.float32)
    real = spectrum[:, :F]
    imag = spectrum[:, F:]
    power = real * real + imag * imag
    high = power.astype(jnp.bfloat16)
    low = (power - high.astype(jnp.float32)).astype(jnp.bfloat16)
    band = band_ref[...]
    mean = jnp.dot(high, band, preferred_element_type=jnp.float32) + jnp.dot(
        low, band, preferred_element_type=jnp.float32
    )
    factor = lax.rsqrt(mean + 1e-05)
    real = real * factor
    imag = imag * factor
    for chunk in range(F // CHUNK):
        lanes = slice(chunk * CHUNK, (chunk + 1) * CHUNK)
        white = jnp.concatenate([real[:, lanes], imag[:, lanes]], axis=1)
        out_ref[chunk] = white.astype(jnp.bfloat16).reshape(BATCH, W, 2 * CHUNK)


def whiten(recorded, source):
    outgoing = source.shape[0]

    def picked(place):
        return pl.BlockSpec((1, W, L), lambda g, src: (src[g * BATCH + place], 0, 0))

    return pl.pallas_call(
        whiten_kernel,
        grid_spec=pltpu.PrefetchScalarGridSpec(
            num_scalar_prefetch=1,
            grid=(outgoing // BATCH,),
            in_specs=[picked(place) for place in range(BATCH)]
            + [
                pl.BlockSpec((L, 2 * F), lambda g, src: (0, 0)),
                pl.BlockSpec((F, F), lambda g, src: (0, 0)),
            ],
            out_specs=pl.BlockSpec(
                (F // CHUNK, BATCH, W, 2 * CHUNK), lambda g, src: (0, g, 0, 0)
            ),
        ),
        out_shape=jax.ShapeDtypeStruct((F // CHUNK, outgoing, W, 2 * CHUNK), jnp.bfloat16),
        compiler_params=pltpu.CompilerParams(vmem_limit_bytes=48 * 1024 * 1024),
    )(source, *[recorded] * BATCH, jnp.asarray(transform_table()), jnp.asarray(band_means()))


def flipped(value, bit):
    return value + (1 << bit) * (1 - 2 * ((value // (1 << bit)) % 2))


def masked(value, mask):
    bit = 0
    while mask >> bit:
        if (mask >> bit) & 1:
            value = flipped(value, bit)
        bit += 1
    return value


def gather_kernel(
    rows, cols, owned, white_ref, tag_ref, mask_ref, real_ref, imag_ref,
    left, right, turnpad, arrived, tags, mixed, wide_mask, local_sem, swap_send, swap_recv, tag_send, tag_recv, cube_send, cube_recv, up_send, up_recv, down_send, down_recv,
):
    row = lax.axis_index("row")
    col = lax.axis_index("col")
    bits = cols.bit_length() - 1
    chunks = F // CHUNK
    depth = CHUNK * owned
    stations = cols * owned
    across = rows * owned
    orders = ([*range(1, bits), 0], [*range(2, bits), 1, 0])

    def span(chunk, half):
        first = HEAD + chunk * depth + half * (depth // 2)
        if half == 0 and chunk == 0:
            return pl.ds(0, HEAD + depth // 2)
        return pl.ds(first, depth // 2)

    def cube_copies(chunk, stage):
        copies = []
        for half in range(2):
            order = orders[half]
            partner = flipped(col, order[stage])
            for member in range(1 << stage):
                mask = 0
                for place in range(stage):
                    if (member >> place) & 1:
                        mask |= 1 << order[place]
                block = masked(col, mask)
                index = (1 << stage) - 1 + member
                ref = left.at[block, span(chunk, half), :]
                copies.append(
                    pltpu.make_async_remote_copy(
                        src_ref=ref,
                        dst_ref=ref,
                        send_sem=cube_send.at[chunk, half, index],
                        recv_sem=cube_recv.at[chunk, half, index],
                        device_id=(row, partner),
                        device_id_type=MESH,
                    )
                )
        return copies

    def line_copy(chunk, stage, up, half):
        step = 1 if up else -1
        block = row - step * stage
        block = jnp.clip(block, 0, rows - 1)
        ref = right.at[block, span(chunk, half), :]
        send, recv = (up_send, up_recv) if up else (down_send, down_recv)
        return pltpu.make_async_remote_copy(
            src_ref=ref,
            dst_ref=ref,
            send_sem=send.at[chunk, half, stage],
            recv_sem=recv.at[chunk, half, stage],
            device_id=(jnp.clip(row + step, 0, rows - 1), col),
            device_id_type=MESH,
        )

    def line_arrival(chunk, stage, up, half):
        step = 1 if up else -1
        block = jnp.clip(row - step * (stage + 1), 0, rows - 1)
        ref = right.at[block, span(chunk, half), :]
        send, recv = (up_send, up_recv) if up else (down_send, down_recv)
        return pltpu.make_async_remote_copy(
            src_ref=ref,
            dst_ref=ref,
            send_sem=send.at[chunk, half, stage],
            recv_sem=recv.at[chunk, half, stage],
            device_id=(jnp.clip(row + step, 0, rows - 1), col),
            device_id_type=MESH,
        )

    def sends(stage, up):
        if up:
            return jnp.logical_and(row - stage >= 0, row + 1 < rows)
        return jnp.logical_and(row + stage < rows, row >= 1)

    def receives(stage, up):
        if up:
            return row - 1 - stage >= 0
        return row + 1 + stage < rows

    def start_cube(chunk, stage):
        for copy in cube_copies(chunk, stage):
            copy.start()

    def land_cube(chunk, stage):
        for copy in cube_copies(chunk, stage):
            copy.wait_recv()

    def start_line(chunk, stage, half):
        for up in (True, False):
            @pl.when(sends(stage, up))
            def _():
                line_copy(chunk, stage, up, half).start()

    def land_line(chunk, stage, half):
        for up in (True, False):
            @pl.when(receives(stage, up))
            def _():
                line_arrival(chunk, stage, up, half).wait_recv()

    own = []
    for chunk in range(chunks):
        own.append(
            pltpu.make_async_copy(
                white_ref.at[chunk, col], arrived.at[chunk, col], local_sem.at[2, chunk]
            )
        )
    own.append(pltpu.make_async_copy(tag_ref.at[col], tags.at[col], local_sem.at[0, 1]))
    for copy in own:
        copy.start()

    barrier = pltpu.get_barrier_semaphore()
    for member in range(1, cols):
        pl.semaphore_signal(
            barrier, inc=1, device_id=(row, masked(col, member)), device_id_type=MESH
        )

    @pl.when(row + 1 < rows)
    def _():
        pl.semaphore_signal(barrier, inc=1, device_id=(row + 1, col), device_id_type=MESH)

    @pl.when(row >= 1)
    def _():
        pl.semaphore_signal(barrier, inc=1, device_id=(row - 1, col), device_id_type=MESH)

    inner = jnp.logical_and(row + 1 < rows, row >= 1)
    pl.semaphore_wait(barrier, cols - 1 + jnp.where(inner, 2, 1))

    def tag_copy(member, landing):
        partner = masked(col, member)
        return pltpu.make_async_remote_copy(
            src_ref=tag_ref.at[partner],
            dst_ref=tags.at[partner if landing else col],
            send_sem=tag_send.at[member - 1],
            recv_sem=tag_recv.at[member - 1],
            device_id=(row, partner),
            device_id_type=MESH,
        )

    def swap_copy(chunk, member, landing):
        partner = masked(col, member)
        return pltpu.make_async_remote_copy(
            src_ref=white_ref.at[chunk, partner],
            dst_ref=arrived.at[chunk, partner if landing else col],
            send_sem=swap_send.at[chunk, member - 1],
            recv_sem=swap_recv.at[chunk, member - 1],
            device_id=(row, partner),
            device_id_type=MESH,
        )

    for member in range(1, cols):
        tag_copy(member, False).start()
    for member in range(1, cols):
        swap_copy(0, member, False).start()
    lone = mask_ref[...].astype(jnp.float32)
    window = jnp.concatenate([lone, lone], axis=1)
    wide_mask[...] = window
    header = jnp.concatenate([window, jnp.zeros((HEAD - owned, 2 * W), jnp.float32)], axis=0)
    left[col, 0:HEAD, :] = header.astype(jnp.bfloat16)
    right[row, 0:HEAD, :] = header.astype(jnp.bfloat16)
    for copy in own:
        copy.wait()

    def prepare(chunk):
        for member in range(1, cols):
            if chunk == 0:
                tag_copy(member, True).wait_recv()
            swap_copy(chunk, member, True).wait_recv()
        if chunk + 1 < chunks:
            for member in range(1, cols):
                swap_copy(chunk + 1, member, False).start()
        names = [tags[c].astype(jnp.float32) for c in range(cols)]
        names = [names[c][rank : rank + 1, :] for c in range(cols) for rank in range(CAP)]

        def choose(station, carry):
            name = station.astype(jnp.float32)
            total = jnp.zeros((W, 2 * CHUNK), jnp.float32)
            for slot in range(cols * CAP):
                weight = jnp.where(names[slot] == name, 1.0, 0.0)
                weight = jnp.concatenate([weight, weight], axis=1)
                total += arrived[chunk, slot // CAP, slot % CAP].astype(jnp.float32) * weight
            both = jnp.concatenate([total[:, :CHUNK], total[:, CHUNK:]], axis=0)
            mixed[pl.ds(station, CHUNK, stride=owned), :] = both.T * wide_mask[pl.ds(station, 1), :]
            return carry

        lax.fori_loop(0, owned, choose, 0)
        block = mixed[...].astype(jnp.bfloat16)
        at = pl.ds(HEAD + chunk * depth, depth)
        left[col, at, :] = block
        right[row, at, :] = block

    lane = lax.broadcasted_iota(jnp.int32, (across, 2 * W), 1)
    sign = jnp.where(lane < W, 1.0, -1.0)
    empty = jnp.zeros((2 * across, 2 * W), jnp.bfloat16)
    half_cols = cols // 2
    half_stations = stations // 2
    planes = 4 * across // 128

    def paired(lefts, both):
        low = jnp.concatenate(lefts[:half_cols], axis=0)
        high = jnp.concatenate(lefts[half_cols:], axis=0)
        one = jnp.concatenate([low, high], axis=1).astype(jnp.bfloat16)
        both = both.astype(jnp.bfloat16)
        wide = jnp.concatenate(
            [
                jnp.concatenate([both, empty], axis=1),
                jnp.concatenate([empty, both], axis=1),
            ],
            axis=0,
        )
        return lax.dot_general(
            one, wide, (((1,), (1,)), ((), ())), preferred_element_type=jnp.float32
        )

    def inverse_counts():
        lefts = [left[c, 0:HEAD, :].astype(jnp.float32)[:owned] for c in range(cols)]
        rights = [right[r, 0:HEAD, :].astype(jnp.float32)[:owned] for r in range(rows)]
        counts = paired(lefts, jnp.concatenate(rights * 2, axis=0))
        return 1.0 / jnp.maximum(0.5 * counts, 1.0)

    def compute(chunk):
        inverse = inverse_counts()
        first = HEAD + chunk * depth

        def group(index, carry):
            at = pl.ds(pl.multiple_of(first + index * GROUP * owned, GROUP * owned // 4), GROUP * owned)
            lefts = [left[c, at, :].astype(jnp.float32) for c in range(cols)]
            rights = [right[r, at, :].astype(jnp.float32) for r in range(rows)]
            for which in range(GROUP):
                rows_of = slice(which * owned, (which + 1) * owned)
                plain = jnp.concatenate([v[rows_of] for v in rights], axis=0)
                turned = pltpu.roll(plain, W, 1) * sign
                product = paired(
                    [v[rows_of] for v in lefts], jnp.concatenate([plain, turned], axis=0)
                )
                put = pl.multiple_of((index * GROUP + which) * half_stations, half_stations)
                scaled = product * inverse
                for plane in range(planes):
                    turnpad[plane, pl.ds(put, half_stations), :] = scaled[
                        :, plane * 128 : (plane + 1) * 128
                    ]
            return carry

        lax.fori_loop(0, CHUNK // GROUP, group, 0)

        def station(index, carry):
            block = jnp.concatenate(
                [
                    turnpad[plane, pl.ds(index, CHUNK, stride=half_stations), :].T
                    for plane in range(planes)
                ],
                axis=0,
            )
            lanes = pl.ds(chunk * CHUNK, CHUNK)
            for half in range(2):
                base = half * 2 * across
                put = index + half * half_stations
                real_ref[put, :, lanes] = block[base : base + across].astype(jnp.bfloat16)
                imag_ref[put, :, lanes] = block[base + across : base + 2 * across].astype(
                    jnp.bfloat16
                )
            return carry

        lax.fori_loop(0, half_stations, station, 0, unroll=4)

    line_stages = rows - 1
    stages = max(bits, line_stages)
    for slot in range(chunks + stages):
        for stage in range(stages, -1, -1):
            chunk = slot - stage
            if chunk < 0 or chunk >= chunks:
                continue
            if stage == 0:
                prepare(chunk)
            for half in range(2):
                if 1 <= stage <= line_stages:
                    land_line(chunk, stage - 1, half)
                if stage < line_stages:
                    start_line(chunk, stage, half)
            if 1 <= stage <= bits:
                land_cube(chunk, stage - 1)
            if stage < bits:
                start_cube(chunk, stage)
        done = slot - stages
        if 0 <= done < chunks:
            compute(done)

    for member in range(1, cols):
        tag_copy(member, False).wait_send()
        for chunk in range(chunks):
            swap_copy(chunk, member, False).wait_send()
    for chunk in range(chunks):
        for stage in range(bits):
            for copy in cube_copies(chunk, stage):
                copy.wait_send()
        for stage in range(line_stages):
            for up in (True, False):
                @pl.when(sends(stage, up))
                def _():
                    line_copy(chunk, stage, up, 0).wait_send()
                    line_copy(chunk, stage, up, 1).wait_send()


def cross_spectra(white, tags, mask, owned):
    rows = lax.axis_size("row")
    cols = lax.axis_size("col")
    stations = cols * owned
    across = rows * owned
    chunks = F // CHUNK
    shape = jax.ShapeDtypeStruct((stations, across, F), jnp.bfloat16)
    depth = HEAD + F * owned
    return pl.pallas_call(
        functools.partial(gather_kernel, rows, cols, owned),
        out_shape=(shape, shape),
        in_specs=[pl.BlockSpec(memory_space=pl.ANY)] * 2
        + [pl.BlockSpec(memory_space=pltpu.VMEM)],
        out_specs=[pl.BlockSpec(memory_space=pltpu.VMEM)] * 2,
        scratch_shapes=[
            pltpu.VMEM((cols, depth, 2 * W), jnp.bfloat16),
            pltpu.VMEM((rows, depth, 2 * W), jnp.bfloat16),
            pltpu.VMEM((4 * across // 128, CHUNK * stations // 2, 128), jnp.float32),
            pltpu.VMEM((chunks, cols, CAP, W, 2 * CHUNK), jnp.bfloat16),
            pltpu.VMEM((cols, HEAD, 2 * W), jnp.bfloat16),
            pltpu.VMEM((CHUNK * owned, 2 * W), jnp.float32),
            pltpu.VMEM((owned, 2 * W), jnp.float32),
            pltpu.SemaphoreType.DMA((3, max(chunks, 2))),
            pltpu.SemaphoreType.DMA((chunks, cols - 1)),
            pltpu.SemaphoreType.DMA((chunks, cols - 1)),
            pltpu.SemaphoreType.DMA((cols - 1,)),
            pltpu.SemaphoreType.DMA((cols - 1,)),
            pltpu.SemaphoreType.DMA((chunks, 2, cols - 1)),
            pltpu.SemaphoreType.DMA((chunks, 2, cols - 1)),
            pltpu.SemaphoreType.DMA((chunks, 2, rows - 1)),
            pltpu.SemaphoreType.DMA((chunks, 2, rows - 1)),
            pltpu.SemaphoreType.DMA((chunks, 2, rows - 1)),
            pltpu.SemaphoreType.DMA((chunks, 2, rows - 1)),
        ],
        compiler_params=pltpu.CompilerParams(
            collective_id=0, has_side_effects=True, vmem_limit_bytes=56 * 1024 * 1024
        ),
        cost_estimate=pl.CostEstimate(
            flops=4 * F * stations * across * 2 * W, bytes_accessed=20_000_000, transcendentals=0
        ),
    )(white, tags, mask)


def per_device(recorded, seg_count, slot_station, window_mask):
    columns = lax.axis_size("col")
    slots_here = recorded.shape[0]
    owned = window_mask.shape[0]
    outgoing = columns * CAP
    slot_index = jnp.arange(slots_here, dtype=jnp.int32)
    live = slot_index < seg_count[0]
    target_col = jnp.where(live, slot_station // owned % columns, columns)
    onehot = (target_col[:, None] == jnp.arange(columns, dtype=jnp.int32)[None, :]).astype(
        jnp.int32
    )
    earlier = jnp.cumsum(onehot, axis=0) - onehot
    rank = jnp.sum(earlier * onehot, axis=1)
    position = jnp.where(live, target_col * CAP + rank, outgoing)
    chosen = position[None, :] == jnp.arange(outgoing, dtype=jnp.int32)[:, None]
    source = jnp.sum(jnp.where(chosen, slot_index[None, :], 0), axis=1)
    local_id = jnp.sum(jnp.where(chosen, slot_station[None, :] % owned + 1, 0), axis=1) - 1
    labels = local_id.astype(jnp.bfloat16).reshape(columns, CAP, 1)
    labels = jnp.broadcast_to(jnp.pad(labels, ((0, 0), (0, HEAD - CAP), (0, 0))), (columns, HEAD, 2 * W))
    white = whiten(recorded, source.astype(jnp.int32))
    white = white.reshape(F // CHUNK, columns, CAP, W, 2 * CHUNK)
    return cross_spectra(white, labels, window_mask, owned)


def solution(mesh):
    placed = (
        P(("row", "col"), None, None),
        P(("row", "col")),
        P(("row", "col")),
        P(("row", "col"), None),
    )
    return jax.shard_map(
        per_device,
        mesh=mesh,
        in_specs=placed,
        out_specs=(P("row", "col", None), P("row", "col", None)),
        check_vma=False,
    )
```

```python
import functools
import math

import jax
import jax.numpy as jnp
import numpy as np
from jax import lax
from jax.experimental import pallas as pl
from jax.experimental.pallas import tpu as pltpu
from jax.sharding import PartitionSpec as P

F = 384
L = 3072
F0 = 13
BAND = 64
CAP = 2
W = 64
CHUNK = 128
HEAD = 16
GROUP = 8
BATCH = 8
PIECES = 3
MESH = pl.DeviceIdType.MESH


def transform_table():
    times = np.arange(L, dtype=np.int64)
    freqs = np.arange(F, dtype=np.int64) + F0
    phase = times[:, None] * freqs[None, :] % L
    angle = phase.astype(np.float64) * (2.0 * math.pi / L)
    return np.concatenate([np.cos(angle), -np.sin(angle)], axis=1).astype(jnp.bfloat16)


def band_means():
    band = np.arange(F) // BAND
    return ((band[:, None] == band[None, :]) / BAND).astype(jnp.bfloat16)


def whiten_kernel(source_ref, *refs):
    segments = jnp.concatenate([ref[0] for ref in refs[:BATCH]], axis=0)
    table_ref, band_ref, out_ref = refs[BATCH:]
    spectrum = jnp.dot(segments, table_ref[...], preferred_element_type=jnp.float32)
    real = spectrum[:, :F]
    imag = spectrum[:, F:]
    power = real * real + imag * imag
    high = power.astype(jnp.bfloat16)
    low = (power - high.astype(jnp.float32)).astype(jnp.bfloat16)
    band = band_ref[...]
    mean = jnp.dot(high, band, preferred_element_type=jnp.float32) + jnp.dot(
        low, band, preferred_element_type=jnp.float32
    )
    factor = lax.rsqrt(mean + 1e-05)
    real = real * factor
    imag = imag * factor
    for chunk in range(F // CHUNK):
        lanes = slice(chunk * CHUNK, (chunk + 1) * CHUNK)
        white = jnp.concatenate([real[:, lanes], imag[:, lanes]], axis=1)
        out_ref[chunk] = white.astype(jnp.bfloat16).reshape(BATCH, W, 2 * CHUNK)


def whiten(recorded, source):
    outgoing = source.shape[0]

    def picked(place):
        return pl.BlockSpec((1, W, L), lambda g, src: (src[g * BATCH + place], 0, 0))

    return pl.pallas_call(
        whiten_kernel,
        grid_spec=pltpu.PrefetchScalarGridSpec(
            num_scalar_prefetch=1,
            grid=(outgoing // BATCH,),
            in_specs=[picked(place) for place in range(BATCH)]
            + [
                pl.BlockSpec((L, 2 * F), lambda g, src: (0, 0)),
                pl.BlockSpec((F, F), lambda g, src: (0, 0)),
            ],
            out_specs=pl.BlockSpec(
                (F // CHUNK, BATCH, W, 2 * CHUNK), lambda g, src: (0, g, 0, 0)
            ),
        ),
        out_shape=jax.ShapeDtypeStruct((F // CHUNK, outgoing, W, 2 * CHUNK), jnp.bfloat16),
        compiler_params=pltpu.CompilerParams(vmem_limit_bytes=48 * 1024 * 1024),
    )(source, *[recorded] * BATCH, jnp.asarray(transform_table()), jnp.asarray(band_means()))


def flipped(value, bit):
    return value + (1 << bit) * (1 - 2 * ((value // (1 << bit)) % 2))


def masked(value, mask):
    bit = 0
    while mask >> bit:
        if (mask >> bit) & 1:
            value = flipped(value, bit)
        bit += 1
    return value


def gather_kernel(
    rows, cols, owned, white_ref, tag_ref, mask_ref, real_ref, imag_ref,
    left, right, turnpad, arrived, tags, mixed, wide_mask, local_sem, swap_send, swap_recv, tag_send, tag_recv, cube_send, cube_recv, up_send, up_recv, down_send, down_recv,
):
    row = lax.axis_index("row")
    col = lax.axis_index("col")
    bits = cols.bit_length() - 1
    chunks = F // CHUNK
    depth = CHUNK * owned
    stations = cols * owned
    across = rows * owned
    orders = ([*range(1, bits), 0], [*range(2, bits), 1, 0])

    def span(chunk, half):
        first = HEAD + chunk * depth + half * (depth // 2)
        if half == 0 and chunk == 0:
            return pl.ds(0, HEAD + depth // 2)
        return pl.ds(first, depth // 2)

    def cube_copies(chunk, stage):
        copies = []
        for half in range(2):
            order = orders[half]
            partner = flipped(col, order[stage])
            for member in range(1 << stage):
                mask = 0
                for place in range(stage):
                    if (member >> place) & 1:
                        mask |= 1 << order[place]
                block = masked(col, mask)
                index = (1 << stage) - 1 + member
                ref = left.at[block, span(chunk, half), :]
                copies.append(
                    pltpu.make_async_remote_copy(
                        src_ref=ref,
                        dst_ref=ref,
                        send_sem=cube_send.at[chunk, half, index],
                        recv_sem=cube_recv.at[chunk, half, index],
                        device_id=(row, partner),
                        device_id_type=MESH,
                    )
                )
        return copies

    def line_copy(chunk, stage, up, half):
        step = 1 if up else -1
        block = row - step * stage
        block = jnp.clip(block, 0, rows - 1)
        ref = right.at[block, span(chunk, half), :]
        send, recv = (up_send, up_recv) if up else (down_send, down_recv)
        return pltpu.make_async_remote_copy(
            src_ref=ref,
            dst_ref=ref,
            send_sem=send.at[chunk, half, stage],
            recv_sem=recv.at[chunk, half, stage],
            device_id=(jnp.clip(row + step, 0, rows - 1), col),
            device_id_type=MESH,
        )

    def line_arrival(chunk, stage, up, half):
        step = 1 if up else -1
        block = jnp.clip(row - step * (stage + 1), 0, rows - 1)
        ref = right.at[block, span(chunk, half), :]
        send, recv = (up_send, up_recv) if up else (down_send, down_recv)
        return pltpu.make_async_remote_copy(
            src_ref=ref,
            dst_ref=ref,
            send_sem=send.at[chunk, half, stage],
            recv_sem=recv.at[chunk, half, stage],
            device_id=(jnp.clip(row + step, 0, rows - 1), col),
            device_id_type=MESH,
        )

    def sends(stage, up):
        if up:
            return jnp.logical_and(row - stage >= 0, row + 1 < rows)
        return jnp.logical_and(row + stage < rows, row >= 1)

    def receives(stage, up):
        if up:
            return row - 1 - stage >= 0
        return row + 1 + stage < rows

    def start_cube(chunk, stage):
        for copy in cube_copies(chunk, stage):
            copy.start()

    def land_cube(chunk, stage):
        for copy in cube_copies(chunk, stage):
            copy.wait_recv()

    def start_line(chunk, stage, half):
        for up in (True, False):
            @pl.when(sends(stage, up))
            def _():
                line_copy(chunk, stage, up, half).start()

    def land_line(chunk, stage, half):
        for up in (True, False):
            @pl.when(receives(stage, up))
            def _():
                line_arrival(chunk, stage, up, half).wait_recv()

    own = []
    for chunk in range(chunks):
        own.append(
            pltpu.make_async_copy(
                white_ref.at[chunk, col], arrived.at[chunk, col], local_sem.at[2, chunk]
            )
        )
    own.append(pltpu.make_async_copy(tag_ref.at[col], tags.at[col], local_sem.at[0, 1]))
    for copy in own:
        copy.start()

    barrier = pltpu.get_barrier_semaphore()
    for member in range(1, cols):
        pl.semaphore_signal(
            barrier, inc=1, device_id=(row, masked(col, member)), device_id_type=MESH
        )

    @pl.when(row + 1 < rows)
    def _():
        pl.semaphore_signal(barrier, inc=1, device_id=(row + 1, col), device_id_type=MESH)

    @pl.when(row >= 1)
    def _():
        pl.semaphore_signal(barrier, inc=1, device_id=(row - 1, col), device_id_type=MESH)

    inner = jnp.logical_and(row + 1 < rows, row >= 1)
    pl.semaphore_wait(barrier, cols - 1 + jnp.where(inner, 2, 1))

    def tag_copy(member, landing):
        partner = masked(col, member)
        return pltpu.make_async_remote_copy(
            src_ref=tag_ref.at[partner],
            dst_ref=tags.at[partner if landing else col],
            send_sem=tag_send.at[member - 1],
            recv_sem=tag_recv.at[member - 1],
            device_id=(row, partner),
            device_id_type=MESH,
        )

    def swap_copy(chunk, member, landing):
        partner = masked(col, member)
        return pltpu.make_async_remote_copy(
            src_ref=white_ref.at[chunk, partner],
            dst_ref=arrived.at[chunk, partner if landing else col],
            send_sem=swap_send.at[chunk, member - 1],
            recv_sem=swap_recv.at[chunk, member - 1],
            device_id=(row, partner),
            device_id_type=MESH,
        )

    for member in range(1, cols):
        tag_copy(member, False).start()
    for member in range(1, cols):
        swap_copy(0, member, False).start()
    lone = mask_ref[...].astype(jnp.float32)
    window = jnp.concatenate([lone, lone], axis=1)
    wide_mask[...] = window
    header = jnp.concatenate([window, jnp.zeros((HEAD - owned, 2 * W), jnp.float32)], axis=0)
    left[col, 0:HEAD, :] = header.astype(jnp.bfloat16)
    right[row, 0:HEAD, :] = header.astype(jnp.bfloat16)
    for copy in own:
        copy.wait()

    def prepare(chunk):
        for member in range(1, cols):
            if chunk == 0:
                tag_copy(member, True).wait_recv()
            swap_copy(chunk, member, True).wait_recv()
        if chunk + 1 < chunks:
            for member in range(1, cols):
                swap_copy(chunk + 1, member, False).start()
        names = [tags[c].astype(jnp.float32) for c in range(cols)]
        names = [names[c][rank : rank + 1, :] for c in range(cols) for rank in range(CAP)]

        def choose(station, carry):
            name = station.astype(jnp.float32)
            total = jnp.zeros((W, 2 * CHUNK), jnp.float32)
            for slot in range(cols * CAP):
                weight = jnp.where(names[slot] == name, 1.0, 0.0)
                weight = jnp.concatenate([weight, weight], axis=1)
                total += arrived[chunk, slot // CAP, slot % CAP].astype(jnp.float32) * weight
            both = jnp.concatenate([total[:, :CHUNK], total[:, CHUNK:]], axis=0)
            mixed[pl.ds(station, CHUNK, stride=owned), :] = both.T * wide_mask[pl.ds(station, 1), :]
            return carry

        lax.fori_loop(0, owned, choose, 0)
        block = mixed[...].astype(jnp.bfloat16)
        at = pl.ds(HEAD + chunk * depth, depth)
        left[col, at, :] = block
        right[row, at, :] = block

    lane = lax.broadcasted_iota(jnp.int32, (across, 2 * W), 1)
    sign = jnp.where(lane < W, 1.0, -1.0)
    empty = jnp.zeros((2 * across, 2 * W), jnp.bfloat16)
    half_cols = cols // 2
    half_stations = stations // 2
    planes = 4 * across // 128

    def paired(lefts, both):
        low = jnp.concatenate(lefts[:half_cols], axis=0)
        high = jnp.concatenate(lefts[half_cols:], axis=0)
        one = jnp.concatenate([low, high], axis=1).astype(jnp.bfloat16)
        both = both.astype(jnp.bfloat16)
        wide = jnp.concatenate(
            [
                jnp.concatenate([both, empty], axis=1),
                jnp.concatenate([empty, both], axis=1),
            ],
            axis=0,
        )
        return lax.dot_general(
            one, wide, (((1,), (1,)), ((), ())), preferred_element_type=jnp.float32
        )

    def inverse_counts():
        lefts = [left[c, 0:HEAD, :].astype(jnp.float32)[:owned] for c in range(cols)]
        rights = [right[r, 0:HEAD, :].astype(jnp.float32)[:owned] for r in range(rows)]
        counts = paired(lefts, jnp.concatenate(rights * 2, axis=0))
        return 1.0 / jnp.maximum(0.5 * counts, 1.0)

    def compute(chunk, piece):
        inverse = inverse_counts()
        first = HEAD + chunk * depth

        def group(index, carry):
            at = pl.ds(pl.multiple_of(first + index * GROUP * owned, GROUP * owned // 4), GROUP * owned)
            lefts = [left[c, at, :].astype(jnp.float32) for c in range(cols)]
            rights = [right[r, at, :].astype(jnp.float32) for r in range(rows)]
            for which in range(GROUP):
                rows_of = slice(which * owned, (which + 1) * owned)
                plain = jnp.concatenate([v[rows_of] for v in rights], axis=0)
                turned = pltpu.roll(plain, W, 1) * sign
                product = paired(
                    [v[rows_of] for v in lefts], jnp.concatenate([plain, turned], axis=0)
                )
                put = pl.multiple_of((index * GROUP + which) * half_stations, half_stations)
                scaled = product * inverse
                for plane in range(planes):
                    turnpad[plane, pl.ds(put, half_stations), :] = scaled[
                        :, plane * 128 : (plane + 1) * 128
                    ]
            return carry

        steps = CHUNK // GROUP
        if piece < 2:
            lax.fori_loop(piece * steps // 2, (piece + 1) * steps // 2, group, 0)

        def station(index, carry):
            block = jnp.concatenate(
                [
                    turnpad[plane, pl.ds(index, CHUNK, stride=half_stations), :].T
                    for plane in range(planes)
                ],
                axis=0,
            )
            lanes = pl.ds(chunk * CHUNK, CHUNK)
            for half in range(2):
                base = half * 2 * across
                put = index + half * half_stations
                real_ref[put, :, lanes] = block[base : base + across].astype(jnp.bfloat16)
                imag_ref[put, :, lanes] = block[base + across : base + 2 * across].astype(
                    jnp.bfloat16
                )
            return carry

        if piece == 2:
            lax.fori_loop(0, half_stations, station, 0, unroll=4)

    line_stages = rows - 1
    stages = max(bits, line_stages)

    def advance(chunk, stage):
        for half in range(2):
            if stage < line_stages:
                land_line(chunk, stage, half)
            if stage + 1 < line_stages:
                start_line(chunk, stage + 1, half)
        if stage < bits:
            land_cube(chunk, stage)
        if stage + 1 < bits:
            start_cube(chunk, stage + 1)

    def begin(chunk):
        prepare(chunk)
        for half in range(2):
            start_line(chunk, 0, half)
        start_cube(chunk, 0)

    begin(0)
    for chunk in range(chunks):
        for stage in range(stages):
            if chunk >= 1 and stage < PIECES:
                compute(chunk - 1, stage)
            if stage == stages - 1 and chunk + 1 < chunks:
                begin(chunk + 1)
            advance(chunk, stage)
        if chunk >= 1:
            for piece in range(stages, PIECES):
                compute(chunk - 1, piece)
    for piece in range(PIECES):
        compute(chunks - 1, piece)

    for member in range(1, cols):
        tag_copy(member, False).wait_send()
        for chunk in range(chunks):
            swap_copy(chunk, member, False).wait_send()
    for chunk in range(chunks):
        for stage in range(bits):
            for copy in cube_copies(chunk, stage):
                copy.wait_send()
        for stage in range(line_stages):
            for up in (True, False):
                @pl.when(sends(stage, up))
                def _():
                    line_copy(chunk, stage, up, 0).wait_send()
                    line_copy(chunk, stage, up, 1).wait_send()


def cross_spectra(white, tags, mask, owned):
    rows = lax.axis_size("row")
    cols = lax.axis_size("col")
    stations = cols * owned
    across = rows * owned
    chunks = F // CHUNK
    shape = jax.ShapeDtypeStruct((stations, across, F), jnp.bfloat16)
    depth = HEAD + F * owned
    return pl.pallas_call(
        functools.partial(gather_kernel, rows, cols, owned),
        out_shape=(shape, shape),
        in_specs=[pl.BlockSpec(memory_space=pl.ANY)] * 2
        + [pl.BlockSpec(memory_space=pltpu.VMEM)],
        out_specs=[pl.BlockSpec(memory_space=pltpu.VMEM)] * 2,
        scratch_shapes=[
            pltpu.VMEM((cols, depth, 2 * W), jnp.bfloat16),
            pltpu.VMEM((rows, depth, 2 * W), jnp.bfloat16),
            pltpu.VMEM((4 * across // 128, CHUNK * stations // 2, 128), jnp.float32),
            pltpu.VMEM((chunks, cols, CAP, W, 2 * CHUNK), jnp.bfloat16),
            pltpu.VMEM((cols, HEAD, 2 * W), jnp.bfloat16),
            pltpu.VMEM((CHUNK * owned, 2 * W), jnp.float32),
            pltpu.VMEM((owned, 2 * W), jnp.float32),
            pltpu.SemaphoreType.DMA((3, max(chunks, 2))),
            pltpu.SemaphoreType.DMA((chunks, cols - 1)),
            pltpu.SemaphoreType.DMA((chunks, cols - 1)),
            pltpu.SemaphoreType.DMA((cols - 1,)),
            pltpu.SemaphoreType.DMA((cols - 1,)),
            pltpu.SemaphoreType.DMA((chunks, 2, cols - 1)),
            pltpu.SemaphoreType.DMA((chunks, 2, cols - 1)),
            pltpu.SemaphoreType.DMA((chunks, 2, rows - 1)),
            pltpu.SemaphoreType.DMA((chunks, 2, rows - 1)),
            pltpu.SemaphoreType.DMA((chunks, 2, rows - 1)),
            pltpu.SemaphoreType.DMA((chunks, 2, rows - 1)),
        ],
        compiler_params=pltpu.CompilerParams(
            collective_id=0, has_side_effects=True, vmem_limit_bytes=56 * 1024 * 1024
        ),
        cost_estimate=pl.CostEstimate(
            flops=4 * F * stations * across * 2 * W, bytes_accessed=20_000_000, transcendentals=0
        ),
    )(white, tags, mask)


def per_device(recorded, seg_count, slot_station, window_mask):
    columns = lax.axis_size("col")
    slots_here = recorded.shape[0]
    owned = window_mask.shape[0]
    outgoing = columns * CAP
    slot_index = jnp.arange(slots_here, dtype=jnp.int32)
    live = slot_index < seg_count[0]
    target_col = jnp.where(live, slot_station // owned % columns, columns)
    onehot = (target_col[:, None] == jnp.arange(columns, dtype=jnp.int32)[None, :]).astype(
        jnp.int32
    )
    earlier = jnp.cumsum(onehot, axis=0) - onehot
    rank = jnp.sum(earlier * onehot, axis=1)
    position = jnp.where(live, target_col * CAP + rank, outgoing)
    chosen = position[None, :] == jnp.arange(outgoing, dtype=jnp.int32)[:, None]
    source = jnp.sum(jnp.where(chosen, slot_index[None, :], 0), axis=1)
    local_id = jnp.sum(jnp.where(chosen, slot_station[None, :] % owned + 1, 0), axis=1) - 1
    labels = local_id.astype(jnp.bfloat16).reshape(columns, CAP, 1)
    labels = jnp.broadcast_to(jnp.pad(labels, ((0, 0), (0, HEAD - CAP), (0, 0))), (columns, HEAD, 2 * W))
    white = whiten(recorded, source.astype(jnp.int32))
    white = white.reshape(F // CHUNK, columns, CAP, W, 2 * CHUNK)
    return cross_spectra(white, labels, window_mask, owned)


def solution(mesh):
    placed = (
        P(("row", "col"), None, None),
        P(("row", "col")),
        P(("row", "col")),
        P(("row", "col"), None),
    )
    return jax.shard_map(
        per_device,
        mesh=mesh,
        in_specs=placed,
        out_specs=(P("row", "col", None), P("row", "col", None)),
        check_vma=False,
    )
```

```python
import functools
import math

import jax
import jax.numpy as jnp
import numpy as np
from jax import lax
from jax.experimental import pallas as pl
from jax.experimental.pallas import tpu as pltpu
from jax.sharding import PartitionSpec as P

F = 384
L = 3072
F0 = 13
BAND = 64
CAP = 2
W = 64
CHUNK = 128
HEAD = 16
GROUP = 8
BATCH = 8
PIECES = 3
MESH = pl.DeviceIdType.MESH


def transform_table():
    times = np.arange(L, dtype=np.int64)
    freqs = np.arange(F, dtype=np.int64) + F0
    phase = times[:, None] * freqs[None, :] % L
    angle = phase.astype(np.float64) * (2.0 * math.pi / L)
    parts = np.stack([np.cos(angle), -np.sin(angle)], axis=1).reshape(L, 2, F // CHUNK, CHUNK)
    return parts.transpose(0, 2, 1, 3).reshape(L, 2 * F).astype(jnp.bfloat16)


def band_means():
    band = np.arange(CHUNK) // BAND
    return ((band[:, None] == band[None, :]) / BAND).astype(jnp.bfloat16)


def whiten_kernel(source_ref, *refs):
    segments = jnp.concatenate([ref[0] for ref in refs[:BATCH]], axis=0)
    table_ref, band_ref, out_ref = refs[BATCH:]
    band = band_ref[...]
    for chunk in range(F // CHUNK):
        lanes = slice(chunk * 2 * CHUNK, (chunk + 1) * 2 * CHUNK)
        spectrum = jnp.dot(segments, table_ref[:, lanes], preferred_element_type=jnp.float32)
        real = spectrum[:, :CHUNK]
        imag = spectrum[:, CHUNK:]
        power = real * real + imag * imag
        high = power.astype(jnp.bfloat16)
        low = (power - high.astype(jnp.float32)).astype(jnp.bfloat16)
        mean = jnp.dot(high, band, preferred_element_type=jnp.float32) + jnp.dot(
            low, band, preferred_element_type=jnp.float32
        )
        factor = lax.rsqrt(mean + 1e-05)
        white = jnp.concatenate([real * factor, imag * factor], axis=1)
        out_ref[chunk] = white.astype(jnp.bfloat16).reshape(BATCH, W, 2 * CHUNK)


def whiten(recorded, source):
    outgoing = source.shape[0]

    def picked(place):
        return pl.BlockSpec((1, W, L), lambda g, src: (src[g * BATCH + place], 0, 0))

    return pl.pallas_call(
        whiten_kernel,
        grid_spec=pltpu.PrefetchScalarGridSpec(
            num_scalar_prefetch=1,
            grid=(outgoing // BATCH,),
            in_specs=[picked(place) for place in range(BATCH)]
            + [
                pl.BlockSpec((L, 2 * F), lambda g, src: (0, 0)),
                pl.BlockSpec((CHUNK, CHUNK), lambda g, src: (0, 0)),
            ],
            out_specs=pl.BlockSpec(
                (F // CHUNK, BATCH, W, 2 * CHUNK), lambda g, src: (0, g, 0, 0)
            ),
        ),
        out_shape=jax.ShapeDtypeStruct((F // CHUNK, outgoing, W, 2 * CHUNK), jnp.bfloat16),
        compiler_params=pltpu.CompilerParams(vmem_limit_bytes=48 * 1024 * 1024),
    )(source, *[recorded] * BATCH, jnp.asarray(transform_table()), jnp.asarray(band_means()))


def flipped(value, bit):
    return value + (1 << bit) * (1 - 2 * ((value // (1 << bit)) % 2))


def masked(value, mask):
    bit = 0
    while mask >> bit:
        if (mask >> bit) & 1:
            value = flipped(value, bit)
        bit += 1
    return value


def gather_kernel(
    rows, cols, owned, white_ref, tag_ref, mask_ref, real_ref, imag_ref,
    left, right, turnpad, arrived, tags, mixed, wide_mask, local_sem, swap_send, swap_recv, tag_send, tag_recv, cube_send, cube_recv, up_send, up_recv, down_send, down_recv,
):
    row = lax.axis_index("row")
    col = lax.axis_index("col")
    bits = cols.bit_length() - 1
    chunks = F // CHUNK
    depth = CHUNK * owned
    stations = cols * owned
    across = rows * owned
    orders = ([*range(1, bits), 0], [*range(2, bits), 1, 0])

    def span(chunk, half):
        first = HEAD + chunk * depth + half * (depth // 2)
        if half == 0 and chunk == 0:
            return pl.ds(0, HEAD + depth // 2)
        return pl.ds(first, depth // 2)

    def cube_copies(chunk, stage):
        copies = []
        for half in range(2):
            order = orders[half]
            partner = flipped(col, order[stage])
            for member in range(1 << stage):
                mask = 0
                for place in range(stage):
                    if (member >> place) & 1:
                        mask |= 1 << order[place]
                block = masked(col, mask)
                index = (1 << stage) - 1 + member
                ref = left.at[block, span(chunk, half), :]
                copies.append(
                    pltpu.make_async_remote_copy(
                        src_ref=ref,
                        dst_ref=ref,
                        send_sem=cube_send.at[chunk, half, index],
                        recv_sem=cube_recv.at[chunk, half, index],
                        device_id=(row, partner),
                        device_id_type=MESH,
                    )
                )
        return copies

    def line_copy(chunk, stage, up, half):
        step = 1 if up else -1
        block = row - step * stage
        block = jnp.clip(block, 0, rows - 1)
        ref = right.at[block, span(chunk, half), :]
        send, recv = (up_send, up_recv) if up else (down_send, down_recv)
        return pltpu.make_async_remote_copy(
            src_ref=ref,
            dst_ref=ref,
            send_sem=send.at[chunk, half, stage],
            recv_sem=recv.at[chunk, half, stage],
            device_id=(jnp.clip(row + step, 0, rows - 1), col),
            device_id_type=MESH,
        )

    def line_arrival(chunk, stage, up, half):
        step = 1 if up else -1
        block = jnp.clip(row - step * (stage + 1), 0, rows - 1)
        ref = right.at[block, span(chunk, half), :]
        send, recv = (up_send, up_recv) if up else (down_send, down_recv)
        return pltpu.make_async_remote_copy(
            src_ref=ref,
            dst_ref=ref,
            send_sem=send.at[chunk, half, stage],
            recv_sem=recv.at[chunk, half, stage],
            device_id=(jnp.clip(row + step, 0, rows - 1), col),
            device_id_type=MESH,
        )

    def sends(stage, up):
        if up:
            return jnp.logical_and(row - stage >= 0, row + 1 < rows)
        return jnp.logical_and(row + stage < rows, row >= 1)

    def receives(stage, up):
        if up:
            return row - 1 - stage >= 0
        return row + 1 + stage < rows

    def start_cube(chunk, stage):
        for copy in cube_copies(chunk, stage):
            copy.start()

    def land_cube(chunk, stage):
        for copy in cube_copies(chunk, stage):
            copy.wait_recv()

    def start_line(chunk, stage, half):
        for up in (True, False):
            @pl.when(sends(stage, up))
            def _():
                line_copy(chunk, stage, up, half).start()

    def land_line(chunk, stage, half):
        for up in (True, False):
            @pl.when(receives(stage, up))
            def _():
                line_arrival(chunk, stage, up, half).wait_recv()

    own = []
    for chunk in range(chunks):
        own.append(
            pltpu.make_async_copy(
                white_ref.at[chunk, col], arrived.at[chunk, col], local_sem.at[2, chunk]
            )
        )
    own.append(pltpu.make_async_copy(tag_ref.at[col], tags.at[col], local_sem.at[0, 1]))
    for copy in own:
        copy.start()

    barrier = pltpu.get_barrier_semaphore()
    for member in range(1, cols):
        pl.semaphore_signal(
            barrier, inc=1, device_id=(row, masked(col, member)), device_id_type=MESH
        )

    @pl.when(row + 1 < rows)
    def _():
        pl.semaphore_signal(barrier, inc=1, device_id=(row + 1, col), device_id_type=MESH)

    @pl.when(row >= 1)
    def _():
        pl.semaphore_signal(barrier, inc=1, device_id=(row - 1, col), device_id_type=MESH)

    inner = jnp.logical_and(row + 1 < rows, row >= 1)
    pl.semaphore_wait(barrier, cols - 1 + jnp.where(inner, 2, 1))

    def tag_copy(member, landing):
        partner = masked(col, member)
        return pltpu.make_async_remote_copy(
            src_ref=tag_ref.at[partner],
            dst_ref=tags.at[partner if landing else col],
            send_sem=tag_send.at[member - 1],
            recv_sem=tag_recv.at[member - 1],
            device_id=(row, partner),
            device_id_type=MESH,
        )

    def swap_copy(chunk, member, landing):
        partner = masked(col, member)
        return pltpu.make_async_remote_copy(
            src_ref=white_ref.at[chunk, partner],
            dst_ref=arrived.at[chunk, partner if landing else col],
            send_sem=swap_send.at[chunk, member - 1],
            recv_sem=swap_recv.at[chunk, member - 1],
            device_id=(row, partner),
            device_id_type=MESH,
        )

    for member in range(1, cols):
        tag_copy(member, False).start()
    for member in range(1, cols):
        swap_copy(0, member, False).start()
    lone = mask_ref[...].astype(jnp.float32)
    window = jnp.concatenate([lone, lone], axis=1)
    wide_mask[...] = window
    header = jnp.concatenate([window, jnp.zeros((HEAD - owned, 2 * W), jnp.float32)], axis=0)
    left[col, 0:HEAD, :] = header.astype(jnp.bfloat16)
    right[row, 0:HEAD, :] = header.astype(jnp.bfloat16)
    for copy in own:
        copy.wait()

    def prepare(chunk):
        for member in range(1, cols):
            if chunk == 0:
                tag_copy(member, True).wait_recv()
            swap_copy(chunk, member, True).wait_recv()
        if chunk + 1 < chunks:
            for member in range(1, cols):
                swap_copy(chunk + 1, member, False).start()
        names = [tags[c].astype(jnp.float32) for c in range(cols)]
        names = [names[c][rank : rank + 1, :] for c in range(cols) for rank in range(CAP)]

        def choose(station, carry):
            name = station.astype(jnp.float32)
            total = jnp.zeros((W, 2 * CHUNK), jnp.float32)
            for slot in range(cols * CAP):
                weight = jnp.where(names[slot] == name, 1.0, 0.0)
                weight = jnp.concatenate([weight, weight], axis=1)
                total += arrived[chunk, slot // CAP, slot % CAP].astype(jnp.float32) * weight
            both = jnp.concatenate([total[:, :CHUNK], total[:, CHUNK:]], axis=0)
            mixed[pl.ds(station, CHUNK, stride=owned), :] = both.T * wide_mask[pl.ds(station, 1), :]
            return carry

        lax.fori_loop(0, owned, choose, 0)
        block = mixed[...].astype(jnp.bfloat16)
        at = pl.ds(HEAD + chunk * depth, depth)
        left[col, at, :] = block
        right[row, at, :] = block

    lane = lax.broadcasted_iota(jnp.int32, (across, 2 * W), 1)
    sign = jnp.where(lane < W, 1.0, -1.0)
    empty = jnp.zeros((2 * across, 2 * W), jnp.bfloat16)
    half_cols = cols // 2
    half_stations = stations // 2
    planes = 4 * across // 128

    def paired(lefts, both):
        low = jnp.concatenate(lefts[:half_cols], axis=0)
        high = jnp.concatenate(lefts[half_cols:], axis=0)
        one = jnp.concatenate([low, high], axis=1).astype(jnp.bfloat16)
        both = both.astype(jnp.bfloat16)
        wide = jnp.concatenate(
            [
                jnp.concatenate([both, empty], axis=1),
                jnp.concatenate([empty, both], axis=1),
            ],
            axis=0,
        )
        return lax.dot_general(
            one, wide, (((1,), (1,)), ((), ())), preferred_element_type=jnp.float32
        )

    def inverse_counts():
        lefts = [left[c, 0:HEAD, :].astype(jnp.float32)[:owned] for c in range(cols)]
        rights = [right[r, 0:HEAD, :].astype(jnp.float32)[:owned] for r in range(rows)]
        counts = paired(lefts, jnp.concatenate(rights * 2, axis=0))
        return 1.0 / jnp.maximum(0.5 * counts, 1.0)

    def compute(chunk, piece):
        inverse = inverse_counts()
        first = HEAD + chunk * depth

        def group(index, carry):
            at = pl.ds(pl.multiple_of(first + index * GROUP * owned, GROUP * owned // 4), GROUP * owned)
            lefts = [left[c, at, :].astype(jnp.float32) for c in range(cols)]
            rights = [right[r, at, :].astype(jnp.float32) for r in range(rows)]
            for which in range(GROUP):
                rows_of = slice(which * owned, (which + 1) * owned)
                plain = jnp.concatenate([v[rows_of] for v in rights], axis=0)
                turned = pltpu.roll(plain, W, 1) * sign
                product = paired(
                    [v[rows_of] for v in lefts], jnp.concatenate([plain, turned], axis=0)
                )
                put = pl.multiple_of((index * GROUP + which) * half_stations, half_stations)
                scaled = product * inverse
                for plane in range(planes):
                    turnpad[plane, pl.ds(put, half_stations), :] = scaled[
                        :, plane * 128 : (plane + 1) * 128
                    ]
            return carry

        steps = CHUNK // GROUP
        if piece < 2:
            lax.fori_loop(piece * steps // 2, (piece + 1) * steps // 2, group, 0)

        def station(index, carry):
            block = jnp.concatenate(
                [
                    turnpad[plane, pl.ds(index, CHUNK, stride=half_stations), :].T
                    for plane in range(planes)
                ],
                axis=0,
            )
            lanes = pl.ds(chunk * CHUNK, CHUNK)
            for half in range(2):
                base = half * 2 * across
                put = index + half * half_stations
                real_ref[put, :, lanes] = block[base : base + across].astype(jnp.bfloat16)
                imag_ref[put, :, lanes] = block[base + across : base + 2 * across].astype(
                    jnp.bfloat16
                )
            return carry

        if piece == 2:
            lax.fori_loop(0, half_stations, station, 0, unroll=4)

    line_stages = rows - 1
    stages = max(bits, line_stages)

    def advance(chunk, stage):
        for half in range(2):
            if stage < line_stages:
                land_line(chunk, stage, half)
            if stage + 1 < line_stages:
                start_line(chunk, stage + 1, half)
        if stage < bits:
            land_cube(chunk, stage)
        if stage + 1 < bits:
            start_cube(chunk, stage + 1)

    def begin(chunk):
        prepare(chunk)
        for half in range(2):
            start_line(chunk, 0, half)
        start_cube(chunk, 0)

    begin(0)
    for chunk in range(chunks):
        for stage in range(stages):
            if chunk >= 1 and stage < PIECES:
                compute(chunk - 1, stage)
            if stage == stages - 1 and chunk + 1 < chunks:
                begin(chunk + 1)
            advance(chunk, stage)
        if chunk >= 1:
            for piece in range(stages, PIECES):
                compute(chunk - 1, piece)
    for piece in range(PIECES):
        compute(chunks - 1, piece)

    for member in range(1, cols):
        tag_copy(member, False).wait_send()
        for chunk in range(chunks):
            swap_copy(chunk, member, False).wait_send()
    for chunk in range(chunks):
        for stage in range(bits):
            for copy in cube_copies(chunk, stage):
                copy.wait_send()
        for stage in range(line_stages):
            for up in (True, False):
                @pl.when(sends(stage, up))
                def _():
                    line_copy(chunk, stage, up, 0).wait_send()
                    line_copy(chunk, stage, up, 1).wait_send()


def cross_spectra(white, tags, mask, owned):
    rows = lax.axis_size("row")
    cols = lax.axis_size("col")
    stations = cols * owned
    across = rows * owned
    chunks = F // CHUNK
    shape = jax.ShapeDtypeStruct((stations, across, F), jnp.bfloat16)
    depth = HEAD + F * owned
    return pl.pallas_call(
        functools.partial(gather_kernel, rows, cols, owned),
        out_shape=(shape, shape),
        in_specs=[pl.BlockSpec(memory_space=pl.ANY)] * 2
        + [pl.BlockSpec(memory_space=pltpu.VMEM)],
        out_specs=[pl.BlockSpec(memory_space=pltpu.VMEM)] * 2,
        scratch_shapes=[
            pltpu.VMEM((cols, depth, 2 * W), jnp.bfloat16),
            pltpu.VMEM((rows, depth, 2 * W), jnp.bfloat16),
            pltpu.VMEM((4 * across // 128, CHUNK * stations // 2, 128), jnp.float32),
            pltpu.VMEM((chunks, cols, CAP, W, 2 * CHUNK), jnp.bfloat16),
            pltpu.VMEM((cols, HEAD, 2 * W), jnp.bfloat16),
            pltpu.VMEM((CHUNK * owned, 2 * W), jnp.float32),
            pltpu.VMEM((owned, 2 * W), jnp.float32),
            pltpu.SemaphoreType.DMA((3, max(chunks, 2))),
            pltpu.SemaphoreType.DMA((chunks, cols - 1)),
            pltpu.SemaphoreType.DMA((chunks, cols - 1)),
            pltpu.SemaphoreType.DMA((cols - 1,)),
            pltpu.SemaphoreType.DMA((cols - 1,)),
            pltpu.SemaphoreType.DMA((chunks, 2, cols - 1)),
            pltpu.SemaphoreType.DMA((chunks, 2, cols - 1)),
            pltpu.SemaphoreType.DMA((chunks, 2, rows - 1)),
            pltpu.SemaphoreType.DMA((chunks, 2, rows - 1)),
            pltpu.SemaphoreType.DMA((chunks, 2, rows - 1)),
            pltpu.SemaphoreType.DMA((chunks, 2, rows - 1)),
        ],
        compiler_params=pltpu.CompilerParams(
            collective_id=0, has_side_effects=True, vmem_limit_bytes=56 * 1024 * 1024
        ),
        cost_estimate=pl.CostEstimate(
            flops=4 * F * stations * across * 2 * W, bytes_accessed=20_000_000, transcendentals=0
        ),
    )(white, tags, mask)


def per_device(recorded, seg_count, slot_station, window_mask):
    columns = lax.axis_size("col")
    slots_here = recorded.shape[0]
    owned = window_mask.shape[0]
    outgoing = columns * CAP
    slot_index = jnp.arange(slots_here, dtype=jnp.int32)
    live = slot_index < seg_count[0]
    target_col = jnp.where(live, slot_station // owned % columns, columns)
    onehot = (target_col[:, None] == jnp.arange(columns, dtype=jnp.int32)[None, :]).astype(
        jnp.int32
    )
    earlier = jnp.cumsum(onehot, axis=0) - onehot
    rank = jnp.sum(earlier * onehot, axis=1)
    position = jnp.where(live, target_col * CAP + rank, outgoing)
    chosen = position[None, :] == jnp.arange(outgoing, dtype=jnp.int32)[:, None]
    source = jnp.sum(jnp.where(chosen, slot_index[None, :], 0), axis=1)
    local_id = jnp.sum(jnp.where(chosen, slot_station[None, :] % owned + 1, 0), axis=1) - 1
    labels = local_id.astype(jnp.bfloat16).reshape(columns, CAP, 1)
    labels = jnp.broadcast_to(jnp.pad(labels, ((0, 0), (0, HEAD - CAP), (0, 0))), (columns, HEAD, 2 * W))
    white = whiten(recorded, source.astype(jnp.int32))
    white = white.reshape(F // CHUNK, columns, CAP, W, 2 * CHUNK)
    return cross_spectra(white, labels, window_mask, owned)


def solution(mesh):
    placed = (
        P(("row", "col"), None, None),
        P(("row", "col")),
        P(("row", "col")),
        P(("row", "col"), None),
    )
    return jax.shard_map(
        per_device,
        mesh=mesh,
        in_specs=placed,
        out_specs=(P("row", "col", None), P("row", "col", None)),
        check_vma=False,
    )
```
